512 devices in a mesh: dc: 128 (over y, z, core), tp: 4 (over x).
Axes of the slice: x: 4, y: 4, z: 16, core: 2. Of those that a mesh axis runs over, the one named last changes fastest.
Arguments:
- query_pre: bfloat16 [256, 128, 2048], P(None, 'dc', 'tp'), may hold values from -40 to 40
- key_pre: bfloat16 [256, 128, 512], P(None, 'dc', 'tp'), may hold values from -40 to 40
- values: bfloat16 [256, 128, 512], P(None, 'dc', 'tp'), may hold values from -6 to 6
- grad_out: bfloat16 [256, 128, 2048], P(None, 'dc', 'tp'), may hold values from -40 to 40
- query_gain: bfloat16 [128], replicated, may hold values from 1 to 8
- key_gain: bfloat16 [128], replicated, may hold values from 1 to 8
- doc_units: int32 [128], replicated, may hold values from 1 to 3, as said below
Outputs:
- grad_query: bfloat16 [256, 128, 2048], P(None, 'dc', 'tp')
- grad_key: bfloat16 [256, 128, 512], P(None, 'dc', 'tp')
- grad_values: bfloat16 [256, 128, 512], P(None, 'dc', 'tp')
- grad_query_gain: float32 [128], replicated
- grad_key_gain: float32 [128], replicated
The draws below stay inside these ranges and needn't reach their ends.
Inputs may be any that keep to these rules, and one draw needn't show every extreme that they name: Document i holds doc_units[i] * 128 tokens; the lengths sum to 256; the first two documents hold 1 and 3 units.
All inputs are finite; a program needn't handle non-finite values.
Results may differ from the reference program's by a relative error of at most 0.035.
The reference program's roundings to bfloat16 on the way (of `attention_low` and `grad_scores`) count: a program that leaves them out, or rounds other values in their place, can miss the bound.
Values may be sent and summed in bfloat16 or wider, within the bound.
A program may use at most 64 MiB of HBM per device.

```python
import math
import jax
import jax.numpy as jnp
from jax import lax

HEADS = 16
KV_HEADS = 4
HEAD_DIM = 128
TOK_DEV = 256
TOKENS = 32768
N_DC = 128


def shared_gains(key, gain_top):
    gain_query = jnp.exp(jax.random.uniform(jax.random.fold_in(key, 101), (HEAD_DIM,), jnp.float32, 0.0, math.log(gain_top)))
    gain_key = jnp.exp(jax.random.uniform(jax.random.fold_in(key, 102), (HEAD_DIM,), jnp.float32, 0.0, math.log(gain_top)))
    return (gain_query, gain_key)


def scaled_rows(own, heads, row_top):
    first_key, second_key, third_key = jax.random.split(own, 3)
    shape_full = (TOK_DEV, N_DC, heads, HEAD_DIM)
    column_scale = jnp.exp(jax.random.uniform(second_key, (HEAD_DIM,), jnp.float32, 0.0, math.log(10.0)))
    row_scale = jnp.exp(jax.random.uniform(third_key, (TOK_DEV, N_DC, heads, 1), jnp.float32, 0.0, math.log(row_top)))
    return (first_key, shape_full, column_scale * row_scale / 10.0)


def draw_query_pre(key, part):
    own = jax.random.fold_in(key, 2)
    base_key, shape_full, factor = scaled_rows(own, HEADS, 10.0)
    result = jnp.clip(jax.random.normal(base_key, shape_full, jnp.float32), -4.0, 4.0) * factor
    return result.reshape(TOK_DEV, N_DC, HEADS * HEAD_DIM).astype(jnp.bfloat16)


def draw_key_pre(key, part):
    own = jax.random.fold_in(key, 3)
    base_key, shape_full, factor = scaled_rows(own, KV_HEADS, 10.0)
    result = jnp.clip(jax.random.normal(base_key, shape_full, jnp.float32), -4.0, 4.0) * factor
    return result.reshape(TOK_DEV, N_DC, KV_HEADS * HEAD_DIM).astype(jnp.bfloat16)


def draw_grad_out(key, part):
    own = jax.random.fold_in(key, 4)
    first_key = jax.random.fold_in(own, 0)
    token_ids = (jnp.arange(TOK_DEV)[:, None] * N_DC + jnp.arange(N_DC)[None, :]).astype(jnp.float32)
    shape_full = (TOK_DEV, N_DC, HEADS * HEAD_DIM)
    ramp_up = 1.0 + 2.0 * token_ids / TOKENS
    result = jnp.clip(jax.random.normal(first_key, shape_full, jnp.float32), -4.0, 4.0)
    return (result * ramp_up[:, :, None]).astype(jnp.bfloat16)


def draw_query_gain(key, part):
    gain_top = 1.6
    return shared_gains(key, gain_top)[0].astype(jnp.bfloat16)


def draw_key_gain(key, part):
    gain_top = 1.6
    return shared_gains(key, gain_top)[1].astype(jnp.bfloat16)


def draw_doc_units(key, part):
    own = jax.random.fold_in(key, 11)
    mean_units = TOK_DEV // N_DC
    others = N_DC - 2
    chosen = jax.random.permutation(own, others * mean_units)[:others * (mean_units - 1)]
    extra_units = jnp.zeros((others,), jnp.int32).at[chosen // mean_units].add(1)
    leading = jnp.array([mean_units - 1, mean_units + 1], jnp.int32)
    return jnp.concatenate([leading, 1 + extra_units]).astype(jnp.int32)


def block_levels(own_key, shape, shards, smallest, largest):
    factor_of = 1.0
    for position, parts in shards:
        steps = jax.random.uniform(jax.random.fold_in(jax.random.fold_in(own_key, 6), position), (parts,), jnp.float32, smallest / len(shards), largest / len(shards))
        factor_of = factor_of * jnp.repeat(jnp.exp(steps), shape[position] // parts).reshape((-1,) + (1,) * (len(shape) - 1 - position))
    return factor_of


def gaussian(rng, extent, deviation, bound, pieces=(), held_as=jnp.bfloat16):
    level = block_levels(rng, extent, pieces, -0.22, 0.18) if pieces else 1.0
    values = jax.random.normal(rng, extent, jnp.float32) * deviation * level
    return jnp.minimum(jnp.maximum(values, -bound), bound).astype(held_as)


def setup_inputs(seed: int = 0) -> dict:
    keys = jax.random.split(jax.random.key(seed), 8)
    return {
        "query_pre": draw_query_pre(jax.random.fold_in(keys[7], 71), 0),
        "key_pre": draw_key_pre(jax.random.fold_in(keys[7], 71), 0),
        "values": gaussian(keys[2], (TOK_DEV, N_DC, KV_HEADS * HEAD_DIM), 1.0, 6.0, ((1, 128), (2, 4))),
        "grad_out": draw_grad_out(jax.random.fold_in(keys[7], 71), 0),
        "query_gain": draw_query_gain(jax.random.fold_in(keys[7], 71), 0),
        "key_gain": draw_key_gain(jax.random.fold_in(keys[7], 71), 0),
        "doc_units": draw_doc_units(jax.random.fold_in(keys[7], 71), 0),
    }


EPS = 1e-06
THETA = 1000000.0

def doc_tables(doc_units, unit_count, devices):
    mean_units = unit_count // devices
    starts = (jnp.cumsum(doc_units) - doc_units).astype(jnp.int32)
    unit_ids = jnp.arange(unit_count, dtype=jnp.int32)
    member = (unit_ids[:, None] >= starts[None, :]).astype(jnp.int32)
    doc_of_unit = (lax.optimization_barrier(jnp.sum(member, axis=1)) - 1).astype(jnp.int32)
    doc_ids = jnp.arange(starts.shape[0], dtype=jnp.int32)
    onehot = (doc_of_unit[:, None] == doc_ids[None, :]).astype(jnp.int32)
    unit_start = lax.optimization_barrier(jnp.sum(onehot * starts[None, :], axis=1)).astype(jnp.int32)
    bounds = jnp.arange(devices + 1, dtype=jnp.int32) * mean_units
    first = lax.optimization_barrier(jnp.min(jnp.where(starts[None, :] >= bounds[:, None], starts[None, :], unit_count), axis=1))
    return (doc_of_unit, unit_start, first.astype(jnp.int32))

def window_tables(doc_of_unit, unit_start, first, owner, capacity, devices):
    unit_count = doc_of_unit.shape[0]
    first_unit = lax.dynamic_index_in_dim(first, owner, 0, keepdims=False)
    limit = lax.dynamic_index_in_dim(first, owner + 1, 0, keepdims=False)
    slot_ids = jnp.arange(capacity, dtype=jnp.int32)
    slot_units = first_unit + slot_ids
    slot_valid = slot_units < limit
    clipped = jnp.minimum(slot_units, unit_count - 1)
    picker = (clipped[:, None] == jnp.arange(unit_count, dtype=jnp.int32)[None, :]).astype(jnp.int32)
    slot_docs = lax.optimization_barrier(jnp.sum(picker * doc_of_unit[None, :], axis=1)).astype(jnp.int32)
    slot_start = lax.optimization_barrier(jnp.sum(picker * unit_start[None, :], axis=1)).astype(jnp.int32)
    slot_docs = jnp.where(slot_valid, slot_docs, -1 - slot_ids)
    lanes = jnp.arange(devices, dtype=jnp.int32)
    token_docs = jnp.broadcast_to(slot_docs[:, None], (capacity, devices)).reshape(-1)
    positions = ((slot_units - slot_start)[:, None] * devices + lanes[None, :]).reshape(-1)
    return (first_unit, slot_valid, token_docs, positions)

def rope_tables(positions, width):
    half_width = width // 2
    frequency = jnp.exp(jnp.arange(half_width, dtype=jnp.float32) * (-2.0 * math.log(THETA) / width))
    angle = positions.astype(jnp.float32)[:, None] * frequency[None, :]
    cosines = jnp.cos(angle)
    sine_values = jnp.sin(angle)
    return (jnp.concatenate([cosines, cosines], -1), jnp.concatenate([sine_values, sine_values], -1))

def rotate(inputs, cosines, sine_values):
    half_width = inputs.shape[-1] // 2
    turned = jnp.concatenate([-inputs[..., half_width:], inputs[..., :half_width]], -1)
    return inputs * cosines[:, None, :] + turned * sine_values[:, None, :]

def norm_forward(inputs, gain, cosines, sine_values):
    widened = inputs.astype(jnp.float32)
    inverse = lax.rsqrt(lax.optimization_barrier(jnp.mean(widened * widened, -1, keepdims=True)) + EPS)
    normed = widened * inverse
    rotated = rotate(normed * gain.astype(jnp.float32), cosines, sine_values).astype(jnp.bfloat16)
    return (rotated, normed, inverse)

def norm_backward(grad_rot, normed, inverse, gain, cosines, sine_values):
    turned = rotate(grad_rot.astype(jnp.float32), cosines, -sine_values)
    product = turned * normed
    scaled = turned * gain.astype(jnp.float32)
    grads = inverse * (scaled - normed * lax.optimization_barrier(jnp.mean(scaled * normed, -1, keepdims=True)))
    return (grads.astype(jnp.bfloat16), product)

def group_backward(query_rot, key_rot, value_rows, grad_rows, keep_mask):
    scale_factor = 1.0 / math.sqrt(query_rot.shape[-1])
    query_wide = lax.optimization_barrier(query_rot).astype(jnp.float32)
    key_wide = lax.optimization_barrier(key_rot).astype(jnp.float32)
    value_wide = value_rows.astype(jnp.float32)
    grad_wide = grad_rows.astype(jnp.float32)
    scores = jnp.einsum('qgd,kd->gqk', query_wide, key_wide) * scale_factor
    scores = jnp.where(keep_mask[None], scores, -jnp.inf)
    row_peak = lax.optimization_barrier(jnp.max(scores, -1, keepdims=True))
    exp_terms = jnp.exp(scores - row_peak)
    attention = exp_terms / lax.optimization_barrier(jnp.sum(exp_terms, -1, keepdims=True))
    attention_low = lax.optimization_barrier(attention.astype(jnp.bfloat16)).astype(jnp.float32)
    output = jnp.einsum('gqk,kd->qgd', attention_low, value_wide)
    delta = lax.optimization_barrier(jnp.sum(grad_wide * output, -1))
    grad_value = jnp.einsum('gqk,qgd->kd', attention_low, grad_wide)
    grad_attention = jnp.einsum('qgd,kd->gqk', grad_wide, value_wide)
    grad_scores = (attention * (grad_attention - jnp.transpose(delta)[:, :, None])).astype(jnp.bfloat16)
    grad_scores = lax.optimization_barrier(grad_scores).astype(jnp.float32)
    grad_q = (jnp.einsum('gqk,kd->qgd', grad_scores, key_wide) * scale_factor).astype(jnp.bfloat16)
    grad_k = (jnp.einsum('gqk,qgd->kd', grad_scores, query_wide) * scale_factor).astype(jnp.bfloat16)
    return (grad_q, grad_k, grad_value.astype(jnp.bfloat16))

def reference(query_pre, key_pre, values, grad_out, query_gain, key_gain, doc_units):
    unit_count = TOK_DEV
    devices = N_DC
    capacity = 2 * (unit_count // devices)
    window = capacity * devices
    group_size = HEADS // KV_HEADS
    doc_of_unit, unit_start, first = doc_tables(doc_units, unit_count, devices)

    def padded(array):
        return jnp.concatenate([array, jnp.zeros((capacity,) + array.shape[1:], array.dtype)], 0)
    query_pad = padded(query_pre)
    key_pad = padded(key_pre)
    value_pad = padded(values)
    grad_pad = padded(grad_out)
    token_order = jnp.arange(window, dtype=jnp.int32)

    def owner_step(carry, owner):
        acc_query, acc_key, acc_value, gain_query, gain_key = carry
        first_unit, slot_valid, token_docs, positions = window_tables(doc_of_unit, unit_start, first, owner, capacity, devices)
        keep_mask = (token_docs[:, None] == token_docs[None, :]) & (token_order[:, None] >= token_order[None, :])
        cosines, sine_values = rope_tables(positions, HEAD_DIM)
        query_win = lax.dynamic_slice_in_dim(query_pad, first_unit, capacity, 0).reshape(window, HEADS, HEAD_DIM)
        key_win = lax.dynamic_slice_in_dim(key_pad, first_unit, capacity, 0).reshape(window, KV_HEADS, HEAD_DIM)
        value_win = lax.dynamic_slice_in_dim(value_pad, first_unit, capacity, 0).reshape(window, KV_HEADS, HEAD_DIM)
        grad_win = lax.dynamic_slice_in_dim(grad_pad, first_unit, capacity, 0).reshape(window, KV_HEADS, group_size, HEAD_DIM)
        query_rot, query_hat, query_inv = norm_forward(query_win, query_gain, cosines, sine_values)
        key_rot, key_hat, key_inv = norm_forward(key_win, key_gain, cosines, sine_values)
        grad_qrot, grad_krot, grad_vals = jax.vmap(group_backward, in_axes=(1, 1, 1, 1, None), out_axes=1)(query_rot.reshape(window, KV_HEADS, group_size, HEAD_DIM), key_rot, value_win, grad_win, keep_mask)
        grad_qpre, query_prod = norm_backward(grad_qrot.reshape(window, HEADS, HEAD_DIM), query_hat, query_inv, query_gain, cosines, sine_values)
        grad_kpre, key_prod = norm_backward(grad_krot, key_hat, key_inv, key_gain, cosines, sine_values)
        slot_mask = jnp.broadcast_to(slot_valid[:, None], (capacity, devices)).reshape(-1)
        gain_query = gain_query + lax.optimization_barrier(jnp.sum(jnp.where(slot_mask[:, None, None], query_prod, 0.0), axis=(0, 1)))
        gain_key = gain_key + lax.optimization_barrier(jnp.sum(jnp.where(slot_mask[:, None, None], key_prod, 0.0), axis=(0, 1)))

        def write_rows(accum, fresh):
            fresh = fresh.reshape(capacity, devices, -1)
            old_rows = lax.dynamic_slice_in_dim(accum, first_unit, capacity, 0)
            merged = jnp.where(slot_valid[:, None, None], fresh, old_rows)
            return lax.dynamic_update_slice_in_dim(accum, merged, first_unit, 0)
        acc_query = write_rows(acc_query, grad_qpre)
        acc_key = write_rows(acc_key, grad_kpre)
        acc_value = write_rows(acc_value, grad_vals)
        return ((acc_query, acc_key, acc_value, gain_query, gain_key), None)
    start_carry = (jnp.zeros_like(query_pad), jnp.zeros_like(key_pad), jnp.zeros_like(value_pad), jnp.zeros((HEAD_DIM,), jnp.float32), jnp.zeros((HEAD_DIM,), jnp.float32))
    final_carry, _ = lax.scan(owner_step, start_carry, jnp.arange(devices, dtype=jnp.int32))
    acc_query, acc_key, acc_value, gain_query, gain_key = final_carry
    return (acc_query[:unit_count], acc_key[:unit_count], acc_value[:unit_count], gain_query, gain_key)
```

```python
import math

import jax
import jax.numpy as jnp
from jax import lax
from jax.experimental import pallas as pl
from jax.experimental.pallas import tpu as pltpu
from jax.sharding import PartitionSpec as P

HEADS = 4
DIM = 128
UNIT = 128
EPS = 1e-06
THETA = 1000000.0
SCALE = 1.0 / math.sqrt(DIM)
MASKED = -1e30

NZ = 16
NJ = 8
NX = 4
ROWS = NZ * NJ * 2

K_AT, V_AT, Q_AT, G_AT, FWD = 0, 128, 256, 768, 1280
DQ_AT, DK_AT, DV_AT, BACK = 0, 512, 640, 768
PIECE = 2
PIECES = HEADS // PIECE
WIDE = PIECE * DIM

MESH = pl.DeviceIdType.MESH
F32 = jnp.float32
BF16 = jnp.bfloat16


def dot(a, b, dims):
    return lax.dot_general(a, b, (dims, ((), ())), preferred_element_type=F32)


def swap_halves(x):
    return pltpu.roll(x, DIM // 2, 1)


def kernel(
    q_in, k_in, v_in, g_in, qgain_ref, kgain_ref, docs_ref,
    dq_out, dk_out, dv_out, gain_out,
    r1, s2, r2, s3, r3, s4, kwin, vwin, halo_s, halo_r,
    qrot, qhat, qinv, khat, kinv, prob, dkacc, dvacc, perm, cosw, sinw, gpart,
    gx, gj, gz,
    sem1, sem2, sem3, sem4, semh, semg, send,
):
    me = lax.axis_index("dc")
    x = lax.axis_index("tp")
    y = me // 32
    z = lax.rem(me, 32) // 2
    c = lax.rem(me, 2)
    j = y * 2 + c
    p = z * NJ + j

    def at(yy, zz, cc):
        return (yy * 32 + zz * 2 + cc, x)

    def z_peer(i):
        k = i // 2 + 1
        other = lax.rem(jnp.where(lax.rem(i, 2) == 0, z + k, z + NZ - k), NZ)
        return other, at(y, other, c)

    def j_peer(i):
        other = lax.rem(j + 1 + i, NJ)
        return other, at(other // 2, z, lax.rem(other, 2))

    def x_peer(i):
        other = lax.rem(x + 1 + i, NX)
        return other, (me, other)

    def owner(pp):
        pp = lax.rem(pp + ROWS // 2, ROWS // 2)
        jj = lax.rem(pp, NJ)
        return at(jj // 2, pp // NJ, lax.rem(jj, 2))

    def each(count, body):
        def step(i, carry):
            body(i)
            return carry

        lax.fori_loop(0, count, step, 0)

    def remote(src, dst, send_sem, recv_sem, device):
        pltpu.make_async_remote_copy(
            src_ref=src, dst_ref=dst, send_sem=send_sem, recv_sem=recv_sem,
            device_id=device, device_id_type=MESH,
        ).start()

    def wait(ref, sem):
        pltpu.make_async_copy(ref, ref, sem).wait()

    barrier = pltpu.get_barrier_semaphore()

    def greet(device):
        pl.semaphore_signal(barrier, inc=1, device_id=device, device_id_type=MESH)

    each(NZ - 1, lambda i: greet(z_peer(i)[1]))
    each(NJ - 1, lambda i: greet(j_peer(i)[1]))
    each(NX - 1, lambda i: greet(x_peer(i)[1]))
    greet(owner(p + 1))
    greet(owner(p - 1))
    pl.semaphore_wait(barrier, NZ - 1 + NJ - 1 + NX - 1 + 2)

    sources = [(k_in, 0, K_AT, DIM), (v_in, 0, V_AT, DIM)]
    sources += [(q_in, n * WIDE, Q_AT + n * WIDE, WIDE) for n in range(PIECES)]
    sources += [(g_in, n * WIDE, G_AT + n * WIDE, WIDE) for n in range(PIECES)]
    for n, (ref, start, lane, width) in enumerate(sources):
        here = r1.at[pl.ds(pl.multiple_of(z * 16, 16), 16), pl.ds(lane, width)]

        def block(other, ref=ref, start=start, width=width):
            return ref.at[pl.ds(pl.multiple_of(other * 16, 16), 16), pl.ds(start, width)]

        def go(i, block=block, here=here, n=n):
            other, device = z_peer(i)
            remote(block(other), here, send.at[0], sem1.at[n], device)

        pltpu.make_async_copy(block(z), here, sem1.at[n]).start()
        each(NZ - 1, go)

    row = lax.broadcasted_iota(jnp.int32, (ROWS, ROWS), 0)
    col = lax.broadcasted_iota(jnp.int32, (ROWS, ROWS), 1)
    perm[...] = jnp.where((row % 16) * 16 + row // 16 == col, 1.0, 0.0).astype(BF16)

    lens = jnp.broadcast_to(docs_ref[...].astype(F32), (UNIT, UNIT))
    doc = lax.broadcasted_iota(jnp.int32, (UNIT, UNIT), 0)
    before = lax.broadcasted_iota(jnp.int32, (UNIT, UNIT), 1)
    starts = jnp.sum(jnp.where(before < doc, lens, 0.0), axis=1, keepdims=True)
    unit = [(2 * p + u).astype(F32) for u in range(2)]
    first = [
        jnp.max(jnp.where(starts <= unit[u], starts, 0.0), axis=0, keepdims=True)
        for u in range(2)
    ]

    def token(index):
        jj = index // 16
        return (jj // 2) * 32 + (index % 16) * 2 + jj % 2

    lane = lax.broadcasted_iota(jnp.int32, (UNIT, DIM), 1)
    place = token(lax.broadcasted_iota(jnp.int32, (UNIT, DIM), 0))
    half = DIM // 2
    freq = jnp.exp((lane % half).astype(F32) * (-2.0 * math.log(THETA) / DIM))
    for u in range(2):
        angle = (place.astype(F32) + (unit[u] - first[u]) * UNIT) * freq
        cosw[u * UNIT : (u + 1) * UNIT] = jnp.cos(angle)
        sinw[u * UNIT : (u + 1) * UNIT] = jnp.where(lane < half, -1.0, 1.0) * jnp.sin(angle)

    causal = jnp.where(
        token(lax.broadcasted_iota(jnp.int32, (UNIT, UNIT), 0))
        <= token(lax.broadcasted_iota(jnp.int32, (UNIT, UNIT), 1)),
        0.0,
        MASKED,
    )
    causal = jnp.concatenate([causal] * PIECE, axis=1)
    seen = [
        [jnp.where(first[u] <= unit[u] - back, 0.0, MASKED) for back in (2, 1)]
        for u in range(2)
    ]
    qgain = qgain_ref[...].astype(F32)
    kgain = kgain_ref[...].astype(F32)

    def turn(a):
        return a * cosw[...] + swap_halves(a) * sinw[...]

    def turn_back(a):
        return a * cosw[...] - swap_halves(a) * sinw[...]

    def norm(raw):
        wide = raw.astype(F32)
        inv = lax.rsqrt(jnp.mean(wide * wide, axis=1, keepdims=True) + EPS)
        return wide * inv, inv

    def norm_back(grad, hat, inv, gain):
        turned = turn_back(grad)
        scaled = turned * gain
        out = inv * (scaled - hat * jnp.mean(scaled * hat, axis=1, keepdims=True))
        return out.astype(BF16), jnp.sum(turned * hat, axis=0, keepdims=True)

    def spread(n):
        _, _, lane, width = sources[n]
        lanes = pl.ds(lane, width)
        wait(r1.at[:, lanes], sem1.at[n])
        moved = dot(perm[...], r1[:, lanes], ((1,), (0,))).astype(BF16)
        s2[:, :, lanes] = moved.reshape(16, 16, width)
        here = r2.at[:, pl.ds(pl.multiple_of(j * 16, 16), 16), lanes]

        def go(i):
            other, device = j_peer(i)
            remote(s2.at[pl.ds(other * 2, 2), :, lanes], here, send.at[1], sem2.at[n], device)

        pltpu.make_async_copy(s2.at[pl.ds(j * 2, 2), :, lanes], here, sem2.at[n]).start()
        each(NJ - 1, go)

    def arrived(n):
        _, _, lane, width = sources[n]
        wait(r2.at[:, :, pl.ds(lane, width)], sem2.at[n])

    def give_back(n, lane, width):
        lanes = pl.ds(lane, width)
        here = r3.at[pl.ds(j * 2, 2), :, lanes]

        def block(other):
            return s3.at[:, pl.ds(pl.multiple_of(other * 16, 16), 16), lanes]

        def go(i):
            other, device = j_peer(i)
            remote(block(other), here, send.at[2], sem3.at[n], device)

        pltpu.make_async_copy(block(j), here, sem3.at[n]).start()
        each(NJ - 1, go)

    def send_home(n, lane, width, out, start):
        lanes = pl.ds(lane, width)
        wait(r3.at[:, :, lanes], sem3.at[n])
        moved = dot(perm[...], r3[:, :, lanes].reshape(ROWS, width), ((1,), (0,)))
        s4[:, lanes] = moved.astype(BF16)
        here = out.at[pl.ds(pl.multiple_of(z * 16, 16), 16), pl.ds(start, width)]

        def block(other):
            return s4.at[pl.ds(pl.multiple_of(other * 16, 16), 16), lanes]

        def go(i):
            other, device = z_peer(i)
            remote(block(other), here, send.at[3], sem4.at[n], device)

        pltpu.make_async_copy(block(z), here, sem4.at[n]).start()
        each(NZ - 1, go)

    spread(0)
    spread(1)
    arrived(0)
    hat, inv = norm(r2[:, :, K_AT : K_AT + DIM].reshape(2 * UNIT, DIM))
    khat[...] = hat
    kinv[...] = inv
    kwin[2 * UNIT :] = turn(hat * kgain).astype(BF16)
    following = owner(p + 1)
    preceding = owner(p - 1)
    remote(kwin.at[pl.ds(2 * UNIT, 2 * UNIT)], kwin.at[pl.ds(0, 2 * UNIT)], send.at[4], semh.at[0], following)
    arrived(1)
    vwin[2 * UNIT :] = r2[:, :, V_AT : V_AT + DIM].reshape(2 * UNIT, DIM)
    remote(vwin.at[pl.ds(2 * UNIT, 2 * UNIT)], vwin.at[pl.ds(0, 2 * UNIT)], send.at[5], semh.at[1], following)

    def window(u):
        return slice(u * UNIT, (u + 3) * UNIT)

    def heads(n, u):
        return slice(n * WIDE, (n + 1) * WIDE)

    dkacc[...] = jnp.zeros_like(dkacc)
    dvacc[...] = jnp.zeros_like(dvacc)

    def scores(n):
        arrived(2 + n)
        for i in range(PIECE):
            h = n * PIECE + i
            raw = r2[:, :, Q_AT + h * DIM : Q_AT + (h + 1) * DIM].reshape(2 * UNIT, DIM)
            hat, inv = norm(raw)
            qhat[h] = hat
            qinv[h] = inv
            rot = turn(hat * qgain).astype(BF16)
            for u in range(2):
                qrot[u, h * UNIT : (h + 1) * UNIT] = rot[u * UNIT : (u + 1) * UNIT]
        if n == 0:
            wait(kwin.at[pl.ds(0, 2 * UNIT)], semh.at[0])
        for u in range(2):
            s = dot(kwin[window(u)], qrot[u, heads(n, u)], ((1,), (1,))) * SCALE
            s = jnp.concatenate(
                [
                    s[:UNIT] + seen[u][0],
                    s[UNIT : 2 * UNIT] + seen[u][1],
                    s[2 * UNIT :] + causal,
                ],
                axis=0,
            )
            e = jnp.exp(s - jnp.max(s, axis=0, keepdims=True))
            prob[u, n] = e * (1.0 / jnp.sum(e, axis=0, keepdims=True))

    def gradients(n):
        arrived(2 + PIECES + n)
        if n == 0:
            wait(vwin.at[pl.ds(0, 2 * UNIT)], semh.at[1])
        grads = [[None] * PIECE for _ in range(2)]
        for u in range(2):
            lanes = [G_AT + (n * PIECE + i) * DIM for i in range(PIECE)]
            g = jnp.concatenate([r2[u, :, a : a + DIM] for a in lanes], axis=0)
            att = prob[u, n]
            low = att.astype(BF16)
            datt = dot(vwin[window(u)], g, ((1,), (1,)))
            delta = jnp.sum(low.astype(F32) * datt, axis=0, keepdims=True)
            ds = (att * (datt - delta)).astype(BF16)
            dvacc[window(u)] += dot(low, g, ((1,), (0,)))
            dkacc[window(u)] += dot(ds, qrot[u, heads(n, u)], ((1,), (0,)))
            dq = (dot(ds, kwin[window(u)], ((0,), (0,))) * SCALE).astype(BF16).astype(F32)
            for i in range(PIECE):
                grads[u][i] = dq[i * UNIT : (i + 1) * UNIT]
        total = None
        for i in range(PIECE):
            h = n * PIECE + i
            grad = jnp.concatenate([grads[0][i], grads[1][i]], axis=0)
            out, part = norm_back(grad, qhat[h], qinv[h], qgain)
            s3[:, :, DQ_AT + h * DIM : DQ_AT + (h + 1) * DIM] = out.reshape(2, UNIT, DIM)
            total = part if total is None else total + part
        return total

    for n in range(PIECES):
        spread(2 + n)
        scores(n)

    qpart = None
    for n in range(PIECES):
        spread(2 + PIECES + n)
        if n > 0:
            send_home(n - 1, DQ_AT + (n - 1) * WIDE, WIDE, dq_out, (n - 1) * WIDE)
        part = gradients(n)
        qpart = part if qpart is None else qpart + part
        if n == PIECES - 1:
            halo_s[0] = dvacc[: 2 * UNIT].astype(BF16)
            halo_s[1] = (dkacc[: 2 * UNIT] * SCALE).astype(BF16)
            remote(halo_s, halo_r, send.at[6], semh.at[2], preceding)
        give_back(n, DQ_AT + n * WIDE, WIDE)
    wait(halo_r, semh.at[2])
    dv = dvacc[2 * UNIT :] + halo_r[0].astype(F32)
    s3[:, :, DV_AT:] = dv.astype(BF16).reshape(2, UNIT, DIM)
    give_back(PIECES, DV_AT, DIM)
    dk = dkacc[2 * UNIT :] * SCALE + halo_r[1].astype(F32)
    out, kpart = norm_back(dk.astype(BF16).astype(F32), khat[...], kinv[...], kgain)
    s3[:, :, DK_AT:DV_AT] = out.reshape(2, UNIT, DIM)
    give_back(PIECES + 1, DK_AT, DIM)

    which = lax.broadcasted_iota(jnp.int32, (8, DIM), 0)

    def share(stage, value, slots, mine, count, peer):
        gpart[stage] = value
        slots[mine] = value

        def go(i):
            remote(gpart.at[stage], slots.at[mine], send.at[7 + stage], semg.at[stage], peer(i)[1])

        each(count - 1, go)

    def total(stage, slots, count):
        wait(slots.at[pl.ds(0, count - 1)], semg.at[stage])
        return jnp.sum(slots[...], axis=0)

    own = jnp.where(which == 0, qpart, jnp.where(which == 1, kpart, 0.0))
    share(0, own, gx, x, NX, x_peer)
    last = PIECES - 1
    send_home(last, DQ_AT + last * WIDE, WIDE, dq_out, last * WIDE)
    share(1, total(0, gx, NX), gj, j, NJ, j_peer)
    send_home(PIECES, DV_AT, DIM, dv_out, 0)
    send_home(PIECES + 1, DK_AT, DIM, dk_out, 0)
    share(2, total(1, gj, NJ), gz, z, NZ, z_peer)
    gain_out[...] = total(2, gz, NZ)

    for n in range(PIECES):
        wait(dq_out.at[:, pl.ds(n * WIDE, WIDE)], sem4.at[n])
    wait(dv_out, sem4.at[PIECES])
    wait(dk_out, sem4.at[PIECES + 1])

    wait(r1.at[pl.ds(0, ROWS - 16)], send.at[0])
    wait(s2.at[pl.ds(0, 16 - 2)], send.at[1])
    wait(s3.at[:, pl.ds(0, UNIT - 16)], send.at[2])
    wait(s4.at[pl.ds(0, ROWS - 16)], send.at[3])
    wait(kwin.at[pl.ds(0, 2 * UNIT)], send.at[4])
    wait(vwin.at[pl.ds(0, 2 * UNIT)], send.at[5])
    wait(halo_s, send.at[6])
    wait(gx.at[pl.ds(0, NX - 1)], send.at[7])
    wait(gj.at[pl.ds(0, NJ - 1)], send.at[8])
    wait(gz.at[pl.ds(0, NZ - 1)], send.at[9])


def local(query_pre, key_pre, values, grad_out, query_gain, key_gain, doc_units):
    any_spec = pl.BlockSpec(memory_space=pl.ANY)
    vmem = pl.BlockSpec(memory_space=pltpu.VMEM)
    dma = pltpu.SemaphoreType.DMA
    dq, dk, dv, gains = pl.pallas_call(
        kernel,
        out_shape=[
            jax.ShapeDtypeStruct((ROWS, HEADS * DIM), BF16),
            jax.ShapeDtypeStruct((ROWS, DIM), BF16),
            jax.ShapeDtypeStruct((ROWS, DIM), BF16),
            jax.ShapeDtypeStruct((8, DIM), F32),
        ],
        in_specs=[any_spec] * 4 + [vmem] * 3,
        out_specs=[vmem] * 4,
        scratch_shapes=[
            pltpu.VMEM((ROWS, FWD), BF16),
            pltpu.VMEM((16, 16, FWD), BF16),
            pltpu.VMEM((2, UNIT, FWD), BF16),
            pltpu.VMEM((2, UNIT, BACK), BF16),
            pltpu.VMEM((16, 16, BACK), BF16),
            pltpu.VMEM((ROWS, BACK), BF16),
            pltpu.VMEM((4 * UNIT, DIM), BF16),
            pltpu.VMEM((4 * UNIT, DIM), BF16),
            pltpu.VMEM((2, 2 * UNIT, DIM), BF16),
            pltpu.VMEM((2, 2 * UNIT, DIM), BF16),
            pltpu.VMEM((2, HEADS * UNIT, DIM), BF16),
            pltpu.VMEM((HEADS, 2 * UNIT, DIM), F32),
            pltpu.VMEM((HEADS, 2 * UNIT, 1), F32),
            pltpu.VMEM((2 * UNIT, DIM), F32),
            pltpu.VMEM((2 * UNIT, 1), F32),
            pltpu.VMEM((2, PIECES, 3 * UNIT, WIDE), F32),
            pltpu.VMEM((4 * UNIT, DIM), F32),
            pltpu.VMEM((4 * UNIT, DIM), F32),
            pltpu.VMEM((ROWS, ROWS), BF16),
            pltpu.VMEM((2 * UNIT, DIM), F32),
            pltpu.VMEM((2 * UNIT, DIM), F32),
            pltpu.VMEM((3, 8, DIM), F32),
            pltpu.VMEM((NX, 8, DIM), F32),
            pltpu.VMEM((NJ, 8, DIM), F32),
            pltpu.VMEM((NZ, 8, DIM), F32),
            dma((2 + 2 * PIECES,)),
            dma((2 + 2 * PIECES,)),
            dma((2 + PIECES,)),
            dma((2 + PIECES,)),
            dma((3,)),
            dma((3,)),
            dma((10,)),
        ],
        compiler_params=pltpu.CompilerParams(
            collective_id=0, has_side_effects=True, vmem_limit_bytes=40 * 1024 * 1024
        ),
        cost_estimate=pl.CostEstimate(
            flops=1_300_000_000, bytes_accessed=4_000_000, transcendentals=1_000_000
        ),
    )(
        query_pre[:, 0, :],
        key_pre[:, 0, :],
        values[:, 0, :],
        grad_out[:, 0, :],
        query_gain.reshape(1, DIM),
        key_gain.reshape(1, DIM),
        doc_units.reshape(1, UNIT),
    )
    return dq[:, None, :], dk[:, None, :], dv[:, None, :], gains[0], gains[1]


def solution(mesh):
    token = P(None, "dc", "tp")
    return jax.shard_map(
        local,
        mesh=mesh,
        in_specs=(token, token, token, token, P(), P(), P()),
        out_specs=(token, token, token, P(), P()),
        check_vma=False,
    )
```

```python
import math

import jax
import jax.numpy as jnp
from jax import lax
from jax.experimental import pallas as pl
from jax.experimental.pallas import tpu as pltpu
from jax.sharding import PartitionSpec as P

HEADS = 4
DIM = 128
UNIT = 128
EPS = 1e-06
THETA = 1000000.0
SCALE = 1.0 / math.sqrt(DIM)
MASKED = -1e30

NZ = 16
NJ = 8
NX = 4
AHEAD = 3
ROWS = NZ * NJ * 2

K_AT, V_AT, Q_AT, G_AT, FWD = 0, 128, 256, 768, 1280
DQ_AT, DK_AT, DV_AT, BACK = 0, 512, 640, 768

MESH = pl.DeviceIdType.MESH
F32 = jnp.float32
BF16 = jnp.bfloat16


def dot(a, b, dims):
    return lax.dot_general(a, b, (dims, ((), ())), preferred_element_type=F32)


def swap_halves(x):
    return pltpu.roll(x, DIM // 2, 1)


def kernel(
    q_in, k_in, v_in, g_in, qgain_in, kgain_in, docs_in,
    back_out, gain_out,
    qgain_ref, kgain_ref, docs_ref,
    r1, s2, r2, s3, r3, s4, kwin, vwin, halo_s, halo_r,
    qrot, qhat, qinv, khat, kinv, prob, dkacc, dvacc, perm, cosw, sinw, gpart,
    gx, gj, gz,
    sem1, sem2, sem3, sem4, semh, semg, send, small,
):
    me = lax.axis_index("dc")
    x = lax.axis_index("tp")
    y = me // 32
    z = lax.rem(me, 32) // 2
    c = lax.rem(me, 2)
    j = y * 2 + c
    p = z * NJ + j

    def at(yy, zz, cc):
        return (yy * 32 + zz * 2 + cc, x)

    def z_peer(i):
        i = NZ - 2 - i
        k = i // 2 + 1
        other = jnp.where((i & 1) == 0, z + k, z + NZ - k) & (NZ - 1)
        return other, at(y, other, c)

    def j_peer(i):
        other = (j + 1 + i) & (NJ - 1)
        return other, at(other // 2, z, other & 1)

    def x_peer(i):
        other = (x + 1 + i) & (NX - 1)
        return other, (me, other)

    def owner(pp):
        pp = (pp + ROWS // 2) & (ROWS // 2 - 1)
        jj = pp & (NJ - 1)
        return at(jj // 2, pp // NJ, jj & 1)

    def each(count, body):
        def step(i, carry):
            body(i)
            return carry

        lax.fori_loop(0, count, step, 0)

    def remote(src, dst, send_sem, recv_sem, device):
        pltpu.make_async_remote_copy(
            src_ref=src, dst_ref=dst, send_sem=send_sem, recv_sem=recv_sem,
            device_id=device, device_id_type=MESH,
        ).start()

    def wait(ref, sem):
        pltpu.make_async_copy(ref, ref, sem).wait()

    for n, (src, dst) in enumerate(
        ((qgain_in, qgain_ref), (kgain_in, kgain_ref), (docs_in, docs_ref))
    ):
        pltpu.make_async_copy(src, dst, small.at[n]).start()
    barrier = pltpu.get_barrier_semaphore()

    def greet(device):
        pl.semaphore_signal(barrier, inc=1, device_id=device, device_id_type=MESH)

    each(NZ - 1, lambda i: greet(z_peer(i)[1]))
    each(NJ - 1, lambda i: greet(j_peer(i)[1]))
    each(NX - 1, lambda i: greet(x_peer(i)[1]))
    greet(owner(p + 1))
    greet(owner(p - 1))
    pl.semaphore_wait(barrier, NZ - 1 + NJ - 1 + NX - 1 + 2)

    sources = [(k_in, 0, K_AT, DIM), (v_in, 0, V_AT, DIM)]
    sources += [(q_in, h * DIM, Q_AT + h * DIM, DIM) for h in range(HEADS)]
    sources += [(g_in, h * DIM, G_AT + h * DIM, DIM) for h in range(HEADS)]

    def depart(n):
        ref, start, lane, width = sources[n]
        here = r1.at[pl.ds(pl.multiple_of(z * 16, 16), 16), pl.ds(lane, width)]

        def block(other):
            return ref.at[pl.ds(pl.multiple_of(other * 16, 16), 16), pl.ds(start, width)]

        def go(i):
            other, device = z_peer(i)
            remote(block(other), here, send.at[0], sem1.at[n], device)

        pltpu.make_async_copy(block(z), here, sem1.at[n]).start()
        each(NZ - 1, go)

    for n in range(AHEAD):
        depart(n)

    row = lax.broadcasted_iota(jnp.int32, (ROWS, ROWS), 0)
    col = lax.broadcasted_iota(jnp.int32, (ROWS, ROWS), 1)
    perm[...] = jnp.where((row % 16) * 16 + row // 16 == col, 1.0, 0.0).astype(BF16)

    wait(qgain_ref, small.at[0])
    wait(kgain_ref, small.at[1])
    wait(docs_ref, small.at[2])

    lens = jnp.broadcast_to(docs_ref[...].astype(F32), (UNIT, UNIT))
    doc = lax.broadcasted_iota(jnp.int32, (UNIT, UNIT), 0)
    before = lax.broadcasted_iota(jnp.int32, (UNIT, UNIT), 1)
    starts = jnp.sum(jnp.where(before < doc, lens, 0.0), axis=1, keepdims=True)
    unit = [(2 * p + u).astype(F32) for u in range(2)]
    first = [
        jnp.max(jnp.where(starts <= unit[u], starts, 0.0), axis=0, keepdims=True)
        for u in range(2)
    ]

    def token(index):
        jj = index // 16
        return (jj // 2) * 32 + (index % 16) * 2 + jj % 2

    lane = lax.broadcasted_iota(jnp.int32, (UNIT, DIM), 1)
    place = token(lax.broadcasted_iota(jnp.int32, (UNIT, DIM), 0))
    half = DIM // 2
    freq = jnp.exp((lane % half).astype(F32) * (-2.0 * math.log(THETA) / DIM))
    for u in range(2):
        angle = (place.astype(F32) + (unit[u] - first[u]) * UNIT) * freq
        cosw[u * UNIT : (u + 1) * UNIT] = jnp.cos(angle)
        sinw[u * UNIT : (u + 1) * UNIT] = jnp.where(lane < half, -1.0, 1.0) * jnp.sin(angle)

    causal = jnp.where(
        token(lax.broadcasted_iota(jnp.int32, (UNIT, UNIT), 0))
        <= token(lax.broadcasted_iota(jnp.int32, (UNIT, UNIT), 1)),
        0.0,
        MASKED,
    )
    seen = [
        [jnp.where(first[u] <= unit[u] - back, 0.0, MASKED) for back in (2, 1)]
        for u in range(2)
    ]
    qgain = qgain_ref[...].astype(F32)
    kgain = kgain_ref[...].astype(F32)

    def turn(a):
        return a * cosw[...] + swap_halves(a) * sinw[...]

    def turn_back(a):
        return a * cosw[...] - swap_halves(a) * sinw[...]

    def norm(raw):
        wide = raw.astype(F32)
        inv = lax.rsqrt(jnp.mean(wide * wide, axis=1, keepdims=True) + EPS)
        return wide * inv, inv

    def norm_back(grad, hat, inv, gain):
        turned = turn_back(grad)
        scaled = turned * gain
        out = inv * (scaled - hat * jnp.mean(scaled * hat, axis=1, keepdims=True))
        return out.astype(BF16), jnp.sum(turned * hat, axis=0, keepdims=True)

    def spread(n):
        _, _, lane, width = sources[n]
        lanes = pl.ds(lane, width)
        wait(r1.at[:, lanes], sem1.at[n])
        if n + AHEAD < len(sources):
            depart(n + AHEAD)
        moved = dot(perm[...], r1[:, lanes], ((1,), (0,))).astype(BF16)
        s2[:, :, lanes] = moved.reshape(16, 16, width)
        here = r2.at[:, pl.ds(pl.multiple_of(j * 16, 16), 16), lanes]

        def go(i):
            other, device = j_peer(i)
            remote(s2.at[pl.ds(other * 2, 2), :, lanes], here, send.at[1], sem2.at[n], device)

        pltpu.make_async_copy(s2.at[pl.ds(j * 2, 2), :, lanes], here, sem2.at[n]).start()
        each(NJ - 1, go)

    def arrived(n):
        _, _, lane, width = sources[n]
        wait(r2.at[:, :, pl.ds(lane, width)], sem2.at[n])

    def give_back(n, lane, width):
        lanes = pl.ds(lane, width)
        here = r3.at[pl.ds(j * 2, 2), :, lanes]

        def block(other):
            return s3.at[:, pl.ds(pl.multiple_of(other * 16, 16), 16), lanes]

        def go(i):
            other, device = j_peer(i)
            remote(block(other), here, send.at[2], sem3.at[n], device)

        pltpu.make_async_copy(block(j), here, sem3.at[n]).start()
        each(NJ - 1, go)

    def send_home(n, lane, width):
        lanes = pl.ds(lane, width)
        wait(r3.at[:, :, lanes], sem3.at[n])
        moved = dot(perm[...], r3[:, :, lanes].reshape(ROWS, width), ((1,), (0,)))
        s4[:, lanes] = moved.astype(BF16)
        here = back_out.at[pl.ds(pl.multiple_of(z * 16, 16), 16), lanes]

        def block(other):
            return s4.at[pl.ds(pl.multiple_of(other * 16, 16), 16), lanes]

        def go(i):
            other, device = z_peer(i)
            remote(block(other), here, send.at[3], sem4.at[n], device)

        pltpu.make_async_copy(block(z), here, sem4.at[n]).start()
        each(NZ - 1, go)

    following = owner(p + 1)
    preceding = owner(p - 1)

    def window(u):
        return slice(u * UNIT, (u + 3) * UNIT)

    def head(h):
        return slice(h * DIM, (h + 1) * DIM)

    def keys():
        arrived(0)
        hat, inv = norm(r2[:, :, K_AT : K_AT + DIM].reshape(2 * UNIT, DIM))
        khat[...] = hat
        kinv[...] = inv
        kwin[2 * UNIT :] = turn(hat * kgain).astype(BF16)
        remote(kwin.at[pl.ds(2 * UNIT, 2 * UNIT)], kwin.at[pl.ds(0, 2 * UNIT)], send.at[4], semh.at[0], following)
        arrived(1)
        vwin[2 * UNIT :] = r2[:, :, V_AT : V_AT + DIM].reshape(2 * UNIT, DIM)
        remote(vwin.at[pl.ds(2 * UNIT, 2 * UNIT)], vwin.at[pl.ds(0, 2 * UNIT)], send.at[5], semh.at[1], following)
        dkacc[...] = jnp.zeros_like(dkacc)
        dvacc[...] = jnp.zeros_like(dvacc)

    def scores(h):
        arrived(2 + h)
        raw = r2[:, :, Q_AT + h * DIM : Q_AT + (h + 1) * DIM].reshape(2 * UNIT, DIM)
        hat, inv = norm(raw)
        qhat[h] = hat
        qinv[h] = inv
        rot = turn(hat * qgain).astype(BF16)
        for u in range(2):
            qrot[u, head(h)] = rot[u * UNIT : (u + 1) * UNIT]
        if h == 0:
            wait(kwin.at[pl.ds(0, 2 * UNIT)], semh.at[0])
        for u in range(2):
            s = dot(kwin[window(u)], qrot[u, head(h)], ((1,), (1,))) * SCALE
            s = jnp.concatenate(
                [
                    s[:UNIT] + seen[u][0],
                    s[UNIT : 2 * UNIT] + seen[u][1],
                    s[2 * UNIT :] + causal,
                ],
                axis=0,
            )
            e = jnp.exp(s - jnp.max(s, axis=0, keepdims=True))
            prob[u, h] = e * (1.0 / jnp.sum(e, axis=0, keepdims=True))

    def gradients(h):
        arrived(2 + HEADS + h)
        if h == 0:
            wait(vwin.at[pl.ds(0, 2 * UNIT)], semh.at[1])
        grads = []
        for u in range(2):
            g = r2[u, :, G_AT + h * DIM : G_AT + (h + 1) * DIM]
            att = prob[u, h]
            low = att.astype(BF16)
            datt = dot(vwin[window(u)], g, ((1,), (1,)))
            delta = jnp.sum(low.astype(F32) * datt, axis=0, keepdims=True)
            ds = (att * (datt - delta)).astype(BF16)
            dvacc[window(u)] += dot(low, g, ((1,), (0,)))
            dkacc[window(u)] += dot(ds, qrot[u, head(h)], ((1,), (0,)))
            dq = dot(ds, kwin[window(u)], ((0,), (0,))) * SCALE
            grads.append(dq.astype(BF16).astype(F32))
        if h == HEADS - 1:
            halo_s[0] = dvacc[: 2 * UNIT].astype(BF16)
            halo_s[1] = (dkacc[: 2 * UNIT] * SCALE).astype(BF16)
            remote(halo_s, halo_r, send.at[6], semh.at[2], preceding)
        out, part = norm_back(jnp.concatenate(grads, axis=0), qhat[h], qinv[h], qgain)
        s3[:, :, DQ_AT + h * DIM : DQ_AT + (h + 1) * DIM] = out.reshape(2, UNIT, DIM)
        give_back(h, DQ_AT + h * DIM, DIM)
        return part

    which = lax.broadcasted_iota(jnp.int32, (8, DIM), 0)

    def share(stage, value, slots, mine, count, peer):
        gpart[stage] = value
        slots[mine] = value

        def go(i):
            remote(gpart.at[stage], slots.at[mine], send.at[7 + stage], semg.at[stage], peer(i)[1])

        each(count - 1, go)

    def total(stage, slots, count):
        wait(slots.at[pl.ds(0, count - 1)], semg.at[stage])
        return jnp.sum(slots[...], axis=0)

    q_at, g_at = 2, 2 + HEADS
    spread(0)
    spread(1)
    spread(q_at)
    keys()
    spread(q_at + 1)
    spread(q_at + 2)
    scores(0)
    spread(q_at + 3)
    scores(1)
    spread(g_at)
    scores(2)
    spread(g_at + 1)
    scores(3)
    qpart = gradients(0)
    spread(g_at + 2)
    qpart += gradients(1)
    spread(g_at + 3)
    send_home(0, DQ_AT, DIM)
    qpart += gradients(2)
    send_home(1, DQ_AT + DIM, DIM)
    qpart += gradients(3)
    send_home(2, DQ_AT + 2 * DIM, DIM)

    wait(halo_r, semh.at[2])
    dk = dkacc[2 * UNIT :] * SCALE + halo_r[1].astype(F32)
    out, kpart = norm_back(dk.astype(BF16).astype(F32), khat[...], kinv[...], kgain)
    s3[:, :, DK_AT:DV_AT] = out.reshape(2, UNIT, DIM)
    give_back(HEADS, DK_AT, DIM)
    dv = dvacc[2 * UNIT :] + halo_r[0].astype(F32)
    s3[:, :, DV_AT:] = dv.astype(BF16).reshape(2, UNIT, DIM)
    give_back(HEADS + 1, DV_AT, DIM)
    own = jnp.where(which == 0, qpart, jnp.where(which == 1, kpart, 0.0))
    share(0, own, gx, x, NX, x_peer)
    send_home(3, DQ_AT + 3 * DIM, DIM)
    share(1, total(0, gx, NX), gj, j, NJ, j_peer)
    send_home(HEADS, DK_AT, DIM)
    send_home(HEADS + 1, DV_AT, DIM)
    share(2, total(1, gj, NJ), gz, z, NZ, z_peer)
    gain_out[...] = total(2, gz, NZ)

    for n in range(HEADS + 2):
        wait(back_out.at[:, pl.ds(n * DIM, DIM)], sem4.at[n])

    wait(r1.at[pl.ds(0, ROWS - 16)], send.at[0])
    wait(s2.at[pl.ds(0, 16 - 2)], send.at[1])
    wait(s3.at[:, pl.ds(0, UNIT - 16)], send.at[2])
    wait(s4.at[pl.ds(0, ROWS - 16)], send.at[3])
    wait(kwin.at[pl.ds(0, 2 * UNIT)], send.at[4])
    wait(vwin.at[pl.ds(0, 2 * UNIT)], send.at[5])
    wait(halo_s, send.at[6])
    wait(gx.at[pl.ds(0, NX - 1)], send.at[7])
    wait(gj.at[pl.ds(0, NJ - 1)], send.at[8])
    wait(gz.at[pl.ds(0, NZ - 1)], send.at[9])


def local(query_pre, key_pre, values, grad_out, query_gain, key_gain, doc_units):
    vmem = pl.BlockSpec(memory_space=pltpu.VMEM)
    dma = pltpu.SemaphoreType.DMA
    back, gains = pl.pallas_call(
        kernel,
        out_shape=[
            jax.ShapeDtypeStruct((ROWS, BACK), BF16),
            jax.ShapeDtypeStruct((8, DIM), F32),
        ],
        in_specs=[pl.BlockSpec(memory_space=pltpu.HBM)] * 7,
        out_specs=[vmem] * 2,
        scratch_shapes=[
            pltpu.VMEM((1, DIM), BF16),
            pltpu.VMEM((1, DIM), BF16),
            pltpu.VMEM((1, UNIT), jnp.int32),
            pltpu.VMEM((ROWS, FWD), BF16),
            pltpu.VMEM((16, 16, FWD), BF16),
            pltpu.VMEM((2, UNIT, FWD), BF16),
            pltpu.VMEM((2, UNIT, BACK), BF16),
            pltpu.VMEM((16, 16, BACK), BF16),
            pltpu.VMEM((ROWS, BACK), BF16),
            pltpu.VMEM((4 * UNIT, DIM), BF16),
            pltpu.VMEM((4 * UNIT, DIM), BF16),
            pltpu.VMEM((2, 2 * UNIT, DIM), BF16),
            pltpu.VMEM((2, 2 * UNIT, DIM), BF16),
            pltpu.VMEM((2, HEADS * UNIT, DIM), BF16),
            pltpu.VMEM((HEADS, 2 * UNIT, DIM), F32),
            pltpu.VMEM((HEADS, 2 * UNIT, 1), F32),
            pltpu.VMEM((2 * UNIT, DIM), F32),
            pltpu.VMEM((2 * UNIT, 1), F32),
            pltpu.VMEM((2, HEADS, 3 * UNIT, UNIT), F32),
            pltpu.VMEM((4 * UNIT, DIM), F32),
            pltpu.VMEM((4 * UNIT, DIM), F32),
            pltpu.VMEM((ROWS, ROWS), BF16),
            pltpu.VMEM((2 * UNIT, DIM), F32),
            pltpu.VMEM((2 * UNIT, DIM), F32),
            pltpu.VMEM((3, 8, DIM), F32),
            pltpu.VMEM((NX, 8, DIM), F32),
            pltpu.VMEM((NJ, 8, DIM), F32),
            pltpu.VMEM((NZ, 8, DIM), F32),
            dma((2 + 2 * HEADS,)),
            dma((2 + 2 * HEADS,)),
            dma((2 + HEADS,)),
            dma((2 + HEADS,)),
            dma((3,)),
            dma((3,)),
            dma((10,)),
            dma((3,)),
        ],
        compiler_params=pltpu.CompilerParams(
            collective_id=0, has_side_effects=True, vmem_limit_bytes=63 * 1024 * 1024
        ),
        cost_estimate=pl.CostEstimate(
            flops=1_300_000_000, bytes_accessed=4_000_000, transcendentals=1_000_000
        ),
    )(
        query_pre[:, 0, :],
        key_pre[:, 0, :],
        values[:, 0, :],
        grad_out[:, 0, :],
        query_gain.reshape(1, DIM),
        key_gain.reshape(1, DIM),
        doc_units.reshape(1, UNIT),
    )
    back = back[:, None, :]
    return back[..., :DK_AT], back[..., DK_AT:DV_AT], back[..., DV_AT:], gains[0], gains[1]


def solution(mesh):
    token = P(None, "dc", "tp")
    return jax.shard_map(
        local,
        mesh=mesh,
        in_specs=(token, token, token, token, P(), P(), P()),
        out_specs=(token, token, token, P(), P()),
        check_vma=False,
    )
```

```python
import math

import jax
import jax.numpy as jnp
from jax import lax
from jax.experimental import pallas as pl
from jax.experimental.pallas import tpu as pltpu
from jax.sharding import PartitionSpec as P

HEADS = 4
DIM = 128
UNIT = 128
EPS = 1e-06
THETA = 1000000.0
SCALE = 1.0 / math.sqrt(DIM)
MASKED = -1e30

NZ = 16
NJ = 8
NX = 4
AHEAD = 3
ROWS = NZ * NJ * 2

K_AT, V_AT, Q_AT, G_AT, FWD = 0, 128, 256, 768, 1280
DQ_AT, DK_AT, DV_AT, BACK = 0, 512, 640, 768
HALO = 256

MESH = pl.DeviceIdType.MESH
F32 = jnp.float32
BF16 = jnp.bfloat16


def dot(a, b, dims):
    return lax.dot_general(a, b, (dims, ((), ())), preferred_element_type=F32)


def swap_halves(x):
    return pltpu.roll(x, DIM // 2, 1)


def kernel(
    q_in, k_in, v_in, g_in, qgain_in, kgain_in, docs_in,
    back_out, gain_out,
    qgain_ref, kgain_ref, docs_ref,
    r1, s2, r2, s3, r3, s4, kraw, vraw, h3, hr3, kwin, vwin,
    qrot, qhat, qinv, khat, prob, dkacc, dvacc, perm, cosw, sinw, gpart,
    home_k, home_hat, home_inv, home_cos, home_sin,
    gx, gj, gz,
    sem1, sem2, sem3, sem4, semh, semg, send, small,
):
    me = lax.axis_index("dc")
    x = lax.axis_index("tp")
    y = me // 32
    z = lax.rem(me, 32) // 2
    c = lax.rem(me, 2)
    j = y * 2 + c
    p = z * NJ + j

    def at(yy, zz, cc):
        return (yy * 32 + zz * 2 + cc, x)

    def z_peer(i):
        i = NZ - 2 - i
        k = i // 2 + 1
        other = jnp.where((i & 1) == 0, z + k, z + NZ - k) & (NZ - 1)
        return other, at(y, other, c)

    def j_peer(i):
        other = (j + 1 + i) & (NJ - 1)
        return other, at(other // 2, z, other & 1)

    def x_peer(i):
        other = (x + 1 + i) & (NX - 1)
        return other, (me, other)

    def owner(pp):
        pp = (pp + ROWS // 2) & (ROWS // 2 - 1)
        jj = pp & (NJ - 1)
        return at(jj // 2, pp // NJ, jj & 1)

    def each(count, body):
        def step(i, carry):
            body(i)
            return carry

        lax.fori_loop(0, count, step, 0)

    def remote(src, dst, send_sem, recv_sem, device):
        pltpu.make_async_remote_copy(
            src_ref=src, dst_ref=dst, send_sem=send_sem, recv_sem=recv_sem,
            device_id=device, device_id_type=MESH,
        ).start()

    def wait(ref, sem):
        pltpu.make_async_copy(ref, ref, sem).wait()

    for n, (src, dst) in enumerate(
        ((qgain_in, qgain_ref), (kgain_in, kgain_ref), (docs_in, docs_ref), (k_in, home_k))
    ):
        pltpu.make_async_copy(src, dst, small.at[n]).start()
    barrier = pltpu.get_barrier_semaphore()

    def greet(device):
        pl.semaphore_signal(barrier, inc=1, device_id=device, device_id_type=MESH)

    each(NZ - 1, lambda i: greet(z_peer(i)[1]))
    each(NJ - 1, lambda i: greet(j_peer(i)[1]))
    each(NX - 1, lambda i: greet(x_peer(i)[1]))
    greet(owner(p + 1))
    greet(owner(p - 1))

    @pl.when(j != 0)
    def _():
        greet(at(0, (z + 1) & (NZ - 1), 0))

    greeted = NZ - 1 + NJ - 1 + NX - 1 + 2
    pl.semaphore_wait(barrier, jnp.where(j == 0, greeted + NJ - 1, greeted))

    sources = [(k_in, 0, K_AT, DIM), (v_in, 0, V_AT, DIM)]
    sources += [(q_in, h * DIM, Q_AT + h * DIM, DIM) for h in range(HEADS)]
    sources += [(g_in, h * DIM, G_AT + h * DIM, DIM) for h in range(HEADS)]

    def depart(n):
        ref, start, lane, width = sources[n]
        here = r1.at[pl.ds(pl.multiple_of(z * 16, 16), 16), pl.ds(lane, width)]

        def block(other):
            return ref.at[pl.ds(pl.multiple_of(other * 16, 16), 16), pl.ds(start, width)]

        def go(i):
            other, device = z_peer(i)
            remote(block(other), here, send.at[0], sem1.at[n], device)

        pltpu.make_async_copy(block(z), here, sem1.at[n]).start()
        each(NZ - 1, go)

    for n in range(AHEAD):
        depart(n)

    row = lax.broadcasted_iota(jnp.int32, (ROWS, ROWS), 0)
    col = lax.broadcasted_iota(jnp.int32, (ROWS, ROWS), 1)
    perm[...] = jnp.where((row % 16) * 16 + row // 16 == col, 1.0, 0.0).astype(BF16)

    wait(qgain_ref, small.at[0])
    wait(kgain_ref, small.at[1])
    wait(docs_ref, small.at[2])
    wait(home_k, small.at[3])

    lens = jnp.broadcast_to(docs_ref[...].astype(F32), (UNIT, UNIT))
    doc = lax.broadcasted_iota(jnp.int32, (UNIT, UNIT), 0)
    before = lax.broadcasted_iota(jnp.int32, (UNIT, UNIT), 1)
    starts = jnp.sum(jnp.where(before < doc, lens, 0.0), axis=1, keepdims=True)
    unit = [(2 * p + u).astype(F32) for u in range(2)]
    first = [
        jnp.max(jnp.where(starts <= unit[u], starts, 0.0), axis=0, keepdims=True)
        for u in range(2)
    ]

    def token(index):
        jj = index // 16
        return (jj // 2) * 32 + (index % 16) * 2 + jj % 2

    lane = lax.broadcasted_iota(jnp.int32, (UNIT, DIM), 1)
    place = token(lax.broadcasted_iota(jnp.int32, (UNIT, DIM), 0))
    half = DIM // 2
    freq = jnp.exp((lane % half).astype(F32) * (-2.0 * math.log(THETA) / DIM))
    sign = jnp.where(lane < half, -1.0, 1.0)
    for w in range(4):
        angle = (place.astype(F32) + (unit[0] + (w - 2.0) - first[w // 3]) * UNIT) * freq
        cosw[w * UNIT : (w + 1) * UNIT] = jnp.cos(angle)
        sinw[w * UNIT : (w + 1) * UNIT] = sign * jnp.sin(angle)

    col = lax.broadcasted_iota(jnp.int32, (UNIT, UNIT), 1)
    upper = jnp.where(doc < col, 1.0, 0.0).astype(BF16)
    starts_row = dot(lens[:8].astype(BF16), upper, ((1,), (0,)))[:1]
    for half_rows in range(2):
        here = slice(half_rows * UNIT, (half_rows + 1) * UNIT)
        units = (doc + half_rows * UNIT).astype(F32)
        begun = jnp.max(jnp.where(starts_row <= units, starts_row, 0.0), axis=1, keepdims=True)
        angle = ((units - begun) * UNIT + me.astype(F32)) * freq
        home_cos[here] = jnp.cos(angle)
        home_sin[here] = sign * jnp.sin(angle)

    causal = jnp.where(
        token(lax.broadcasted_iota(jnp.int32, (UNIT, UNIT), 0))
        <= token(lax.broadcasted_iota(jnp.int32, (UNIT, UNIT), 1)),
        0.0,
        MASKED,
    )
    seen = [
        [jnp.where(first[u] <= unit[u] - back, 0.0, MASKED) for back in (2, 1)]
        for u in range(2)
    ]
    qgain = qgain_ref[...].astype(F32)
    kgain = kgain_ref[...].astype(F32)

    def turn(a, cos, sin):
        return a * cos + swap_halves(a) * sin

    def norm(raw):
        wide = raw.astype(F32)
        inv = lax.rsqrt(jnp.mean(wide * wide, axis=1, keepdims=True) + EPS)
        return wide * inv, inv

    def norm_back(turned, hat, inv, gain):
        scaled = turned * gain
        out = inv * (scaled - hat * jnp.mean(scaled * hat, axis=1, keepdims=True))
        return out.astype(BF16)

    home_hat[...], home_inv[...] = norm(home_k[...])
    own_rows = slice(2 * UNIT, 4 * UNIT)
    own_cos, own_sin = cosw[own_rows], sinw[own_rows]

    def spread(n):
        _, _, lane, width = sources[n]
        lanes = pl.ds(lane, width)
        wait(r1.at[:, lanes], sem1.at[n])
        if n + AHEAD < len(sources):
            depart(n + AHEAD)
        moved = dot(perm[...], r1[:, lanes], ((1,), (0,))).astype(BF16)
        s2[:, :, lanes] = moved.reshape(16, 16, width)
        here = r2.at[:, pl.ds(pl.multiple_of(j * 16, 16), 16), lanes]

        def go(i):
            other, device = j_peer(i)
            remote(s2.at[pl.ds(other * 2, 2), :, lanes], here, send.at[1], sem2.at[n], device)

        pltpu.make_async_copy(s2.at[pl.ds(j * 2, 2), :, lanes], here, sem2.at[n]).start()
        each(NJ - 1, go)

    def arrived(n):
        _, _, lane, width = sources[n]
        wait(r2.at[:, :, pl.ds(lane, width)], sem2.at[n])

    def give_back(n, lane, width):
        lanes = pl.ds(lane, width)
        here = r3.at[pl.ds(j * 2, 2), :, lanes]

        def block(other):
            return s3.at[:, pl.ds(pl.multiple_of(other * 16, 16), 16), lanes]

        def go(i):
            other, device = j_peer(i)
            remote(block(other), here, send.at[2], sem3.at[n], device)

        pltpu.make_async_copy(block(j), here, sem3.at[n]).start()
        each(NJ - 1, go)

    def give_keys_back():
        lanes = pl.ds(DK_AT, HALO)
        here = r3.at[pl.ds(j * 2, 2), :, lanes]
        before = (j + NJ - 1) & (NJ - 1)
        there = hr3.at[pl.ds(before * 2, 2)]
        row = jnp.where(j == 0, z + NZ - 1, z) & (NZ - 1)

        def block(ref, other, width):
            return ref.at[:, pl.ds(pl.multiple_of(other * 16, 16), 16), width]

        def go(i):
            other, device = j_peer(i)
            remote(block(s3, other, lanes), here, send.at[2], sem3.at[HEADS], device)
            remote(block(h3, other, pl.ds(0, HALO)), there, send.at[5], sem3.at[HEADS + 1], at(other // 2, row, other & 1))

        pltpu.make_async_copy(block(s3, j, lanes), here, sem3.at[HEADS]).start()
        own = block(h3, j, pl.ds(0, HALO))

        @pl.when(j == 0)
        def _():
            remote(own, there, send.at[6], sem3.at[HEADS + 1], at(y, row, c))

        @pl.when(j != 0)
        def _():
            pltpu.make_async_copy(own, there, sem3.at[HEADS + 1]).start()

        each(NJ - 1, go)

    def keys_home():
        wait(r3.at[:, :, pl.ds(DK_AT, HALO)], sem3.at[HEADS])
        wait(hr3, sem3.at[HEADS + 1])
        total = dot(perm[...], r3[:, :, DK_AT:].reshape(ROWS, HALO), ((1,), (0,)))
        total += dot(perm[...], hr3[...].reshape(ROWS, HALO), ((1,), (0,)))
        s4[:, DK_AT:] = total.astype(BF16)
        along_z(HEADS, DK_AT, DIM)
        along_z(HEADS + 1, DV_AT, DIM)

    def send_home(n, lane, width):
        lanes = pl.ds(lane, width)
        wait(r3.at[:, :, lanes], sem3.at[n])
        moved = dot(perm[...], r3[:, :, lanes].reshape(ROWS, width), ((1,), (0,)))
        s4[:, lanes] = moved.astype(BF16)
        along_z(n, lane, width)

    def along_z(n, lane, width):
        lanes = pl.ds(lane, width)
        here = back_out.at[pl.ds(pl.multiple_of(z * 16, 16), 16), lanes]

        def block(other):
            return s4.at[pl.ds(pl.multiple_of(other * 16, 16), 16), lanes]

        def go(i):
            other, device = z_peer(i)
            remote(block(other), here, send.at[3], sem4.at[n], device)

        pltpu.make_async_copy(block(z), here, sem4.at[n]).start()
        each(NZ - 1, go)

    following = owner(p + 1)

    def window(u):
        return slice(u * UNIT, (u + 3) * UNIT)

    def head(h):
        return slice(h * DIM, (h + 1) * DIM)

    def keys():
        arrived(0)
        k_here = r2.at[:, :, pl.ds(K_AT, DIM)]
        remote(k_here, kraw, send.at[4], semh.at[0], following)
        arrived(1)
        v_here = r2.at[:, :, pl.ds(V_AT, DIM)]
        remote(v_here, vraw, send.at[7], semh.at[1], following)
        use_keys(k_here[...], own_rows)
        vwin[own_rows] = v_here[...].reshape(2 * UNIT, DIM)
        dkacc[...] = jnp.zeros_like(dkacc)
        dvacc[...] = jnp.zeros_like(dvacc)

    def use_keys(raw, rows):
        hat, _ = norm(raw.reshape(2 * UNIT, DIM))
        khat[rows] = hat
        kwin[rows] = turn(hat * kgain, cosw[rows], sinw[rows]).astype(BF16)

    def scores(h):
        arrived(2 + h)
        raw = r2[:, :, Q_AT + h * DIM : Q_AT + (h + 1) * DIM].reshape(2 * UNIT, DIM)
        hat, inv = norm(raw)
        qhat[h] = hat
        qinv[h] = inv
        rot = turn(hat * qgain, own_cos, own_sin).astype(BF16)
        for u in range(2):
            qrot[u, head(h)] = rot[u * UNIT : (u + 1) * UNIT]
        if h == 0:
            wait(kraw, semh.at[0])
            use_keys(kraw[...], slice(0, 2 * UNIT))
        for u in range(2):
            s = dot(kwin[window(u)], qrot[u, head(h)], ((1,), (1,))) * SCALE
            s = jnp.concatenate(
                [
                    s[:UNIT] + seen[u][0],
                    s[UNIT : 2 * UNIT] + seen[u][1],
                    s[2 * UNIT :] + causal,
                ],
                axis=0,
            )
            e = jnp.exp(s - jnp.max(s, axis=0, keepdims=True))
            prob[u, h] = e * (1.0 / jnp.sum(e, axis=0, keepdims=True))

    def gradients(h):
        arrived(2 + HEADS + h)
        if h == 0:
            wait(vraw, semh.at[1])
            vwin[: 2 * UNIT] = vraw[...].reshape(2 * UNIT, DIM)
        grads = []
        for u in range(2):
            g = r2[u, :, G_AT + h * DIM : G_AT + (h + 1) * DIM]
            att = prob[u, h]
            low = att.astype(BF16)
            datt = dot(vwin[window(u)], g, ((1,), (1,)))
            delta = jnp.sum(low.astype(F32) * datt, axis=0, keepdims=True)
            ds = (att * (datt - delta)).astype(BF16)
            dvacc[window(u)] += dot(low, g, ((1,), (0,)))
            dkacc[window(u)] += dot(ds, qrot[u, head(h)], ((1,), (0,)))
            dq = dot(ds, kwin[window(u)], ((0,), (0,))) * SCALE
            grads.append(dq.astype(BF16).astype(F32))
        turned = turn(jnp.concatenate(grads, axis=0), own_cos, -own_sin)
        out = norm_back(turned, qhat[h], qinv[h], qgain)
        s3[:, :, DQ_AT + h * DIM : DQ_AT + (h + 1) * DIM] = out.reshape(2, UNIT, DIM)
        give_back(h, DQ_AT + h * DIM, DIM)
        if h == HEADS - 1:
            dk = dkacc[...] * SCALE
            low = dk.astype(BF16).reshape(4, UNIT, DIM)
            s3[:, :, DK_AT:DV_AT] = low[2:]
            h3[:, :, :DIM] = low[:2]
            low = dvacc[...].astype(BF16).reshape(4, UNIT, DIM)
            s3[:, :, DV_AT:] = low[2:]
            h3[:, :, DIM:] = low[:2]
            give_keys_back()
            turned_k = turn(dk, cosw[...], -sinw[...])
            gpart[0, 1:2] = jnp.sum(turned_k * khat[...], axis=0, keepdims=True)
        return jnp.sum(turned * qhat[h], axis=0, keepdims=True)

    def share(stage, value, slots, mine, count, peer):
        if value is not None:
            gpart[stage] = value
        slots[mine] = gpart[stage]

        def go(i):
            remote(gpart.at[stage], slots.at[mine], send.at[8 + stage], semg.at[stage], peer(i)[1])

        each(count - 1, go)

    def total(stage, slots, count):
        wait(slots.at[pl.ds(0, count - 1)], semg.at[stage])
        return jnp.sum(slots[...], axis=0)

    q_at, g_at = 2, 2 + HEADS
    spread(0)
    spread(1)
    spread(q_at)
    keys()
    spread(q_at + 1)
    spread(q_at + 2)
    scores(0)
    spread(q_at + 3)
    scores(1)
    spread(g_at)
    scores(2)
    spread(g_at + 1)
    scores(3)
    qpart = gradients(0)
    spread(g_at + 2)
    qpart += gradients(1)
    spread(g_at + 3)
    send_home(0, DQ_AT, DIM)
    qpart += gradients(2)
    send_home(1, DQ_AT + DIM, DIM)
    qpart += gradients(3)
    gpart[0, 0:1] = qpart
    share(0, None, gx, x, NX, x_peer)
    send_home(2, DQ_AT + 2 * DIM, DIM)
    share(1, total(0, gx, NX), gj, j, NJ, j_peer)
    send_home(3, DQ_AT + 3 * DIM, DIM)
    share(2, total(1, gj, NJ), gz, z, NZ, z_peer)
    keys_home()
    for n in range(HEADS + 1):
        wait(back_out.at[:, pl.ds(n * DIM, DIM)], sem4.at[n])
    dk = turn(back_out[:, DK_AT:DV_AT].astype(F32), home_cos[...], -home_sin[...])
    back_out[:, DK_AT:DV_AT] = norm_back(dk, home_hat[...], home_inv[...], kgain)
    gain_out[...] = total(2, gz, NZ)
    wait(back_out.at[:, pl.ds(DV_AT, DIM)], sem4.at[HEADS + 1])

    wait(r1.at[pl.ds(0, ROWS - 16)], send.at[0])
    wait(s2.at[pl.ds(0, 16 - 2)], send.at[1])
    wait(s3.at[:, pl.ds(0, UNIT - 16)], send.at[2])
    wait(s4.at[pl.ds(0, ROWS - 16)], send.at[3])
    wait(kraw, send.at[4])
    wait(hr3.at[pl.ds(0, 16 - 2)], send.at[5])

    @pl.when(j == 0)
    def _():
        wait(hr3.at[pl.ds(0, 2)], send.at[6])

    wait(vraw, send.at[7])
    wait(gx.at[pl.ds(0, NX - 1)], send.at[8])
    wait(gj.at[pl.ds(0, NJ - 1)], send.at[9])
    wait(gz.at[pl.ds(0, NZ - 1)], send.at[10])


def finish(back, gains, dq, dk, dv, gain_q, gain_k, held, held_gains, sems):
    pieces = (
        (back.at[:, pl.ds(DQ_AT, HEADS * DIM)], held.at[:, pl.ds(DQ_AT, HEADS * DIM)], dq),
        (back.at[:, pl.ds(DK_AT, DIM)], held.at[:, pl.ds(DK_AT, DIM)], dk),
        (back.at[:, pl.ds(DV_AT, DIM)], held.at[:, pl.ds(DV_AT, DIM)], dv),
        (gains.at[pl.ds(0, 1)], held_gains.at[pl.ds(0, 1)], gain_q),
        (gains.at[pl.ds(1, 1)], held_gains.at[pl.ds(1, 1)], gain_k),
    )
    arriving = [
        pltpu.make_async_copy(src, mid, sems.at[0, n]) for n, (src, mid, _) in enumerate(pieces)
    ]
    leaving = [
        pltpu.make_async_copy(mid, dst, sems.at[1, n]) for n, (_, mid, dst) in enumerate(pieces)
    ]
    for copy in arriving:
        copy.start()
    for first, second in zip(arriving, leaving):
        first.wait()
        second.start()
    for copy in leaving:
        copy.wait()


def local(query_pre, key_pre, values, grad_out, query_gain, key_gain, doc_units):
    vmem = pl.BlockSpec(memory_space=pltpu.VMEM)
    dma = pltpu.SemaphoreType.DMA
    back, gains = pl.pallas_call(
        kernel,
        out_shape=[
            jax.ShapeDtypeStruct((ROWS, BACK), BF16),
            jax.ShapeDtypeStruct((2, DIM), F32),
        ],
        in_specs=[pl.BlockSpec(memory_space=pltpu.HBM)] * 7,
        out_specs=[vmem] * 2,
        scratch_shapes=[
            pltpu.VMEM((1, DIM), BF16),
            pltpu.VMEM((1, DIM), BF16),
            pltpu.VMEM((1, UNIT), jnp.int32),
            pltpu.VMEM((ROWS, FWD), BF16),
            pltpu.VMEM((16, 16, FWD), BF16),
            pltpu.VMEM((2, UNIT, FWD), BF16),
            pltpu.VMEM((2, UNIT, BACK), BF16),
            pltpu.VMEM((16, 16, BACK), BF16),
            pltpu.VMEM((ROWS, BACK), BF16),
            pltpu.VMEM((2, UNIT, DIM), BF16),
            pltpu.VMEM((2, UNIT, DIM), BF16),
            pltpu.VMEM((2, UNIT, HALO), BF16),
            pltpu.VMEM((16, 16, HALO), BF16),
            pltpu.VMEM((4 * UNIT, DIM), BF16),
            pltpu.VMEM((4 * UNIT, DIM), BF16),
            pltpu.VMEM((2, HEADS * UNIT, DIM), BF16),
            pltpu.VMEM((HEADS, 2 * UNIT, DIM), F32),
            pltpu.VMEM((HEADS, 2 * UNIT, 1), F32),
            pltpu.VMEM((4 * UNIT, DIM), F32),
            pltpu.VMEM((2, HEADS, 3 * UNIT, UNIT), F32),
            pltpu.VMEM((4 * UNIT, DIM), F32),
            pltpu.VMEM((4 * UNIT, DIM), F32),
            pltpu.VMEM((ROWS, ROWS), BF16),
            pltpu.VMEM((4 * UNIT, DIM), F32),
            pltpu.VMEM((4 * UNIT, DIM), F32),
            pltpu.VMEM((3, 2, DIM), F32),
            pltpu.VMEM((ROWS, DIM), BF16),
            pltpu.VMEM((ROWS, DIM), F32),
            pltpu.VMEM((ROWS, 1), F32),
            pltpu.VMEM((ROWS, DIM), F32),
            pltpu.VMEM((ROWS, DIM), F32),
            pltpu.VMEM((NX, 2, DIM), F32),
            pltpu.VMEM((NJ, 2, DIM), F32),
            pltpu.VMEM((NZ, 2, DIM), F32),
            dma((2 + 2 * HEADS,)),
            dma((2 + 2 * HEADS,)),
            dma((2 + HEADS,)),
            dma((2 + HEADS,)),
            dma((2,)),
            dma((3,)),
            dma((11,)),
            dma((4,)),
        ],
        compiler_params=pltpu.CompilerParams(
            collective_id=0, has_side_effects=True, vmem_limit_bytes=63 * 1024 * 1024
        ),
        cost_estimate=pl.CostEstimate(
            flops=1_300_000_000, bytes_accessed=4_000_000, transcendentals=1_000_000
        ),
    )(
        query_pre[:, 0, :],
        key_pre[:, 0, :],
        values[:, 0, :],
        grad_out[:, 0, :],
        query_gain.reshape(1, DIM),
        key_gain.reshape(1, DIM),
        doc_units.reshape(1, UNIT),
    )
    hbm = pl.BlockSpec(memory_space=pltpu.HBM)
    dq, dk, dv, gain_q, gain_k = pl.pallas_call(
        finish,
        out_shape=[
            jax.ShapeDtypeStruct((ROWS, HEADS * DIM), BF16),
            jax.ShapeDtypeStruct((ROWS, DIM), BF16),
            jax.ShapeDtypeStruct((ROWS, DIM), BF16),
            jax.ShapeDtypeStruct((1, DIM), F32),
            jax.ShapeDtypeStruct((1, DIM), F32),
        ],
        in_specs=[hbm] * 2,
        out_specs=[hbm] * 5,
        scratch_shapes=[pltpu.VMEM((ROWS, BACK), BF16), pltpu.VMEM((2, DIM), F32), dma((2, 5))],
    )(back, gains)
    return dq[:, None, :], dk[:, None, :], dv[:, None, :], gain_q[0], gain_k[0]


def solution(mesh):
    token = P(None, "dc", "tp")
    return jax.shard_map(
        local,
        mesh=mesh,
        in_specs=(token, token, token, token, P(), P(), P()),
        out_specs=(token, token, token, P(), P()),
        check_vma=False,
    )
```

```python
import math

import jax
import jax.numpy as jnp
from jax import lax
from jax.experimental import pallas as pl
from jax.experimental.pallas import tpu as pltpu
from jax.sharding import PartitionSpec as P

HEADS = 4
DIM = 128
UNIT = 128
EPS = 1e-06
THETA = 1000000.0
SCALE = 1.0 / math.sqrt(DIM)
MASKED = -1e30

NZ = 16
NJ = 8
NX = 4
AHEAD = 3
ROWS = NZ * NJ * 2

K_AT, V_AT, Q_AT, G_AT, FWD = 0, 128, 256, 768, 1280
DQ_AT, DK_AT, DV_AT, BACK = 0, 512, 640, 768
HALO = 256

MESH = pl.DeviceIdType.MESH
F32 = jnp.float32
BF16 = jnp.bfloat16


def dot(a, b, dims):
    return lax.dot_general(a, b, (dims, ((), ())), preferred_element_type=F32)


def swap_halves(x):
    return pltpu.roll(x, DIM // 2, 1)


def kernel(
    q_in, k_in, v_in, g_in, qgain_in, kgain_in, docs_in,
    back_out, gain_out,
    qgain_ref, kgain_ref, docs_ref,
    r1, s2, r2, s3, r3, s4, kraw, vraw, h3, hr3, kwin, vwin,
    qrot, qhat, qinv, khat, prob, dkacc, dvacc, perm, cosw, sinw, gpart,
    home_k, home_hat, home_inv, home_cos, home_sin,
    gx, gj, gz,
    sem1, sem2, sem3, sem4, semh, semg, send, small,
):
    me = lax.axis_index("dc")
    x = lax.axis_index("tp")
    y = me // 32
    z = lax.rem(me, 32) // 2
    c = lax.rem(me, 2)
    j = y * 2 + c
    p = z * NJ + j

    def at(yy, zz, cc):
        return (yy * 32 + zz * 2 + cc, x)

    def z_peer(i):
        i = NZ - 2 - i
        k = i // 2 + 1
        other = jnp.where((i & 1) == 0, z + k, z + NZ - k) & (NZ - 1)
        return other, at(y, other, c)

    def j_peer(i):
        other = (j + 1 + i) & (NJ - 1)
        return other, at(other // 2, z, other & 1)

    def x_peer(i):
        other = (x + 1 + i) & (NX - 1)
        return other, (me, other)

    def owner(pp):
        pp = (pp + ROWS // 2) & (ROWS // 2 - 1)
        jj = pp & (NJ - 1)
        return at(jj // 2, pp // NJ, jj & 1)

    def each(count, body):
        def step(i, carry):
            body(i)
            return carry

        lax.fori_loop(0, count, step, 0, unroll=True)

    def remote(src, dst, send_sem, recv_sem, device):
        pltpu.make_async_remote_copy(
            src_ref=src, dst_ref=dst, send_sem=send_sem, recv_sem=recv_sem,
            device_id=device, device_id_type=MESH,
        ).start()

    def wait(ref, sem):
        pltpu.make_async_copy(ref, ref, sem).wait()

    for n, (src, dst) in enumerate(
        ((qgain_in, qgain_ref), (kgain_in, kgain_ref), (docs_in, docs_ref), (k_in, home_k))
    ):
        pltpu.make_async_copy(src, dst, small.at[n]).start()
    barrier = pltpu.get_barrier_semaphore()

    def greet(device):
        pl.semaphore_signal(barrier, inc=1, device_id=device, device_id_type=MESH)

    each(NZ - 1, lambda i: greet(z_peer(i)[1]))
    each(NJ - 1, lambda i: greet(j_peer(i)[1]))
    each(NX - 1, lambda i: greet(x_peer(i)[1]))
    greet(owner(p + 1))
    greet(owner(p - 1))

    @pl.when(j != 0)
    def _():
        greet(at(0, (z + 1) & (NZ - 1), 0))

    greeted = NZ - 1 + NJ - 1 + NX - 1 + 2
    pl.semaphore_wait(barrier, jnp.where(j == 0, greeted + NJ - 1, greeted))

    sources = [(k_in, 0, K_AT, DIM), (v_in, 0, V_AT, DIM)]
    sources += [(q_in, h * DIM, Q_AT + h * DIM, 2 * DIM) for h in (0, 2)]
    sources += [(g_in, h * DIM, G_AT + h * DIM, DIM) for h in range(HEADS)]

    def depart(n):
        ref, start, lane, width = sources[n]
        here = r1.at[pl.ds(pl.multiple_of(z * 16, 16), 16), pl.ds(lane, width)]

        def block(other):
            return ref.at[pl.ds(pl.multiple_of(other * 16, 16), 16), pl.ds(start, width)]

        def go(i):
            other, device = z_peer(i)
            remote(block(other), here, send.at[0], sem1.at[n], device)

        pltpu.make_async_copy(block(z), here, sem1.at[n]).start()
        each(NZ - 1, go)

    for n in range(AHEAD):
        depart(n)

    row = lax.broadcasted_iota(jnp.int32, (ROWS, ROWS), 0)
    col = lax.broadcasted_iota(jnp.int32, (ROWS, ROWS), 1)
    perm[...] = jnp.where((row % 16) * 16 + row // 16 == col, 1.0, 0.0).astype(BF16)

    wait(qgain_ref, small.at[0])
    wait(kgain_ref, small.at[1])
    wait(docs_ref, small.at[2])
    wait(home_k, small.at[3])

    lens = jnp.broadcast_to(docs_ref[...].astype(F32), (UNIT, UNIT))
    doc = lax.broadcasted_iota(jnp.int32, (UNIT, UNIT), 0)
    before = lax.broadcasted_iota(jnp.int32, (UNIT, UNIT), 1)
    starts = jnp.sum(jnp.where(before < doc, lens, 0.0), axis=1, keepdims=True)
    unit = [(2 * p + u).astype(F32) for u in range(2)]
    first = [
        jnp.max(jnp.where(starts <= unit[u], starts, 0.0), axis=0, keepdims=True)
        for u in range(2)
    ]

    def token(index):
        jj = index // 16
        return (jj // 2) * 32 + (index % 16) * 2 + jj % 2

    lane = lax.broadcasted_iota(jnp.int32, (UNIT, DIM), 1)
    place = token(lax.broadcasted_iota(jnp.int32, (UNIT, DIM), 0))
    half = DIM // 2
    freq = jnp.exp((lane % half).astype(F32) * (-2.0 * math.log(THETA) / DIM))
    sign = jnp.where(lane < half, -1.0, 1.0)
    for w in range(4):
        angle = (place.astype(F32) + (unit[0] + (w - 2.0) - first[w // 3]) * UNIT) * freq
        cosw[w * UNIT : (w + 1) * UNIT] = jnp.cos(angle)
        sinw[w * UNIT : (w + 1) * UNIT] = sign * jnp.sin(angle)

    col = lax.broadcasted_iota(jnp.int32, (UNIT, UNIT), 1)
    upper = jnp.where(doc < col, 1.0, 0.0).astype(BF16)
    starts_row = dot(lens[:8].astype(BF16), upper, ((1,), (0,)))[:1]
    for half_rows in range(2):
        here = slice(half_rows * UNIT, (half_rows + 1) * UNIT)
        units = (doc + half_rows * UNIT).astype(F32)
        begun = jnp.max(jnp.where(starts_row <= units, starts_row, 0.0), axis=1, keepdims=True)
        angle = ((units - begun) * UNIT + me.astype(F32)) * freq
        home_cos[here] = jnp.cos(angle)
        home_sin[here] = sign * jnp.sin(angle)

    causal = jnp.where(
        token(lax.broadcasted_iota(jnp.int32, (UNIT, UNIT), 0))
        <= token(lax.broadcasted_iota(jnp.int32, (UNIT, UNIT), 1)),
        0.0,
        MASKED,
    )
    seen = [
        [jnp.where(first[u] <= unit[u] - back, 0.0, MASKED) for back in (2, 1)]
        for u in range(2)
    ]
    qgain = qgain_ref[...].astype(F32)
    kgain = kgain_ref[...].astype(F32)

    def turn(a, cos, sin):
        return a * cos + swap_halves(a) * sin

    def norm(raw):
        wide = raw.astype(F32)
        inv = lax.rsqrt(jnp.mean(wide * wide, axis=1, keepdims=True) + EPS)
        return wide * inv, inv

    def norm_back(turned, hat, inv, gain):
        scaled = turned * gain
        out = inv * (scaled - hat * jnp.mean(scaled * hat, axis=1, keepdims=True))
        return out.astype(BF16)

    home_hat[...], home_inv[...] = norm(home_k[...])
    own_rows = slice(2 * UNIT, 4 * UNIT)
    own_cos, own_sin = cosw[own_rows], sinw[own_rows]

    def spread(n):
        _, _, lane, width = sources[n]
        lanes = pl.ds(lane, width)
        wait(r1.at[:, lanes], sem1.at[n])
        if n + AHEAD < len(sources):
            depart(n + AHEAD)
        moved = dot(perm[...], r1[:, lanes], ((1,), (0,))).astype(BF16)
        s2[:, :, lanes] = moved.reshape(16, 16, width)
        here = r2.at[:, pl.ds(pl.multiple_of(j * 16, 16), 16), lanes]

        def go(i):
            other, device = j_peer(i)
            remote(s2.at[pl.ds(other * 2, 2), :, lanes], here, send.at[1], sem2.at[n], device)

        pltpu.make_async_copy(s2.at[pl.ds(j * 2, 2), :, lanes], here, sem2.at[n]).start()
        each(NJ - 1, go)

    def arrived(n):
        _, _, lane, width = sources[n]
        wait(r2.at[:, :, pl.ds(lane, width)], sem2.at[n])

    def give_back(n, lane, width):
        lanes = pl.ds(lane, width)
        here = r3.at[pl.ds(j * 2, 2), :, lanes]

        def block(other):
            return s3.at[:, pl.ds(pl.multiple_of(other * 16, 16), 16), lanes]

        def go(i):
            other, device = j_peer(i)
            remote(block(other), here, send.at[2], sem3.at[n], device)

        pltpu.make_async_copy(block(j), here, sem3.at[n]).start()
        each(NJ - 1, go)

    def give_keys_back():
        lanes = pl.ds(DK_AT, HALO)
        here = r3.at[pl.ds(j * 2, 2), :, lanes]
        before = (j + NJ - 1) & (NJ - 1)
        there = hr3.at[pl.ds(before * 2, 2)]
        row = jnp.where(j == 0, z + NZ - 1, z) & (NZ - 1)

        def block(ref, other, width):
            return ref.at[:, pl.ds(pl.multiple_of(other * 16, 16), 16), width]

        def go(i):
            other, device = j_peer(i)
            remote(block(s3, other, lanes), here, send.at[2], sem3.at[HEADS], device)
            remote(block(h3, other, pl.ds(0, HALO)), there, send.at[5], sem3.at[HEADS + 1], at(other // 2, row, other & 1))

        pltpu.make_async_copy(block(s3, j, lanes), here, sem3.at[HEADS]).start()
        own = block(h3, j, pl.ds(0, HALO))

        @pl.when(j == 0)
        def _():
            remote(own, there, send.at[6], sem3.at[HEADS + 1], at(y, row, c))

        @pl.when(j != 0)
        def _():
            pltpu.make_async_copy(own, there, sem3.at[HEADS + 1]).start()

        each(NJ - 1, go)

    def keys_home():
        wait(r3.at[:, :, pl.ds(DK_AT, HALO)], sem3.at[HEADS])
        wait(hr3, sem3.at[HEADS + 1])
        total = dot(perm[...], r3[:, :, DK_AT:].reshape(ROWS, HALO), ((1,), (0,)))
        total += dot(perm[...], hr3[...].reshape(ROWS, HALO), ((1,), (0,)))
        s4[:, DK_AT:] = total.astype(BF16)
        along_z(HEADS, DK_AT, DIM)
        along_z(HEADS + 1, DV_AT, DIM)

    def send_home(n, lane, width):
        lanes = pl.ds(lane, width)
        wait(r3.at[:, :, lanes], sem3.at[n])
        moved = dot(perm[...], r3[:, :, lanes].reshape(ROWS, width), ((1,), (0,)))
        s4[:, lanes] = moved.astype(BF16)
        along_z(n, lane, width)

    def along_z(n, lane, width):
        lanes = pl.ds(lane, width)
        here = back_out.at[pl.ds(pl.multiple_of(z * 16, 16), 16), lanes]

        def block(other):
            return s4.at[pl.ds(pl.multiple_of(other * 16, 16), 16), lanes]

        def go(i):
            other, device = z_peer(i)
            remote(block(other), here, send.at[3], sem4.at[n], device)

        pltpu.make_async_copy(block(z), here, sem4.at[n]).start()
        each(NZ - 1, go)

    following = owner(p + 1)

    def window(u):
        return slice(u * UNIT, (u + 3) * UNIT)

    def head(h):
        return slice(h * DIM, (h + 1) * DIM)

    def keys():
        arrived(0)
        k_here = r2.at[:, :, pl.ds(K_AT, DIM)]
        remote(k_here, kraw, send.at[4], semh.at[0], following)
        arrived(1)
        v_here = r2.at[:, :, pl.ds(V_AT, DIM)]
        remote(v_here, vraw, send.at[7], semh.at[1], following)
        use_keys(k_here[...], own_rows)
        vwin[own_rows] = v_here[...].reshape(2 * UNIT, DIM)
        dkacc[...] = jnp.zeros_like(dkacc)
        dvacc[...] = jnp.zeros_like(dvacc)

    def use_keys(raw, rows):
        hat, _ = norm(raw.reshape(2 * UNIT, DIM))
        khat[rows] = hat
        kwin[rows] = turn(hat * kgain, cosw[rows], sinw[rows]).astype(BF16)

    def scores(h):
        if h % 2 == 0:
            arrived(2 + h // 2)
        raw = r2[:, :, Q_AT + h * DIM : Q_AT + (h + 1) * DIM].reshape(2 * UNIT, DIM)
        hat, inv = norm(raw)
        qhat[h] = hat
        qinv[h] = inv
        rot = turn(hat * qgain, own_cos, own_sin).astype(BF16)
        for u in range(2):
            qrot[u, head(h)] = rot[u * UNIT : (u + 1) * UNIT]
        if h == 0:
            wait(kraw, semh.at[0])
            use_keys(kraw[...], slice(0, 2 * UNIT))
        for u in range(2):
            s = dot(kwin[window(u)], qrot[u, head(h)], ((1,), (1,))) * SCALE
            s = jnp.concatenate(
                [
                    s[:UNIT] + seen[u][0],
                    s[UNIT : 2 * UNIT] + seen[u][1],
                    s[2 * UNIT :] + causal,
                ],
                axis=0,
            )
            e = jnp.exp(s - jnp.max(s, axis=0, keepdims=True))
            prob[u, h] = e * (1.0 / jnp.sum(e, axis=0, keepdims=True))

    def gradients(h):
        arrived(4 + h)
        if h == 0:
            wait(vraw, semh.at[1])
            vwin[: 2 * UNIT] = vraw[...].reshape(2 * UNIT, DIM)
        grads = []
        for u in range(2):
            g = r2[u, :, G_AT + h * DIM : G_AT + (h + 1) * DIM]
            att = prob[u, h]
            low = att.astype(BF16)
            datt = dot(vwin[window(u)], g, ((1,), (1,)))
            delta = jnp.sum(low.astype(F32) * datt, axis=0, keepdims=True)
            ds = (att * (datt - delta)).astype(BF16)
            dvacc[window(u)] += dot(low, g, ((1,), (0,)))
            dkacc[window(u)] += dot(ds, qrot[u, head(h)], ((1,), (0,)))
            dq = dot(ds, kwin[window(u)], ((0,), (0,))) * SCALE
            grads.append(dq.astype(BF16).astype(F32))
        turned = turn(jnp.concatenate(grads, axis=0), own_cos, -own_sin)
        out = norm_back(turned, qhat[h], qinv[h], qgain)
        s3[:, :, DQ_AT + h * DIM : DQ_AT + (h + 1) * DIM] = out.reshape(2, UNIT, DIM)
        give_back(h, DQ_AT + h * DIM, DIM)
        if h == HEADS - 1:
            dk = dkacc[...] * SCALE
            low = dk.astype(BF16).reshape(4, UNIT, DIM)
            s3[:, :, DK_AT:DV_AT] = low[2:]
            h3[:, :, :DIM] = low[:2]
            low = dvacc[...].astype(BF16).reshape(4, UNIT, DIM)
            s3[:, :, DV_AT:] = low[2:]
            h3[:, :, DIM:] = low[:2]
            give_keys_back()
            turned_k = turn(dk, cosw[...], -sinw[...])
            gpart[0, 1:2] = jnp.sum(turned_k * khat[...], axis=0, keepdims=True)
        return jnp.sum(turned * qhat[h], axis=0, keepdims=True)

    def share(stage, value, slots, mine, count, peer):
        if value is not None:
            gpart[stage] = value
        slots[mine] = gpart[stage]

        def go(i):
            remote(gpart.at[stage], slots.at[mine], send.at[8 + stage], semg.at[stage], peer(i)[1])

        each(count - 1, go)

    def total(stage, slots, count):
        wait(slots.at[pl.ds(0, count - 1)], semg.at[stage])
        return jnp.sum(slots[...], axis=0)

    q_at, g_at = 2, 4
    spread(0)
    spread(1)
    spread(q_at)
    keys()
    spread(q_at + 1)
    scores(0)
    scores(1)
    spread(g_at)
    scores(2)
    scores(3)
    spread(g_at + 1)
    qpart = gradients(0)
    spread(g_at + 2)
    qpart += gradients(1)
    spread(g_at + 3)
    send_home(0, DQ_AT, DIM)
    qpart += gradients(2)
    send_home(1, DQ_AT + DIM, DIM)
    qpart += gradients(3)
    gpart[0, 0:1] = qpart
    share(0, None, gx, x, NX, x_peer)
    send_home(2, DQ_AT + 2 * DIM, DIM)
    share(1, total(0, gx, NX), gj, j, NJ, j_peer)
    send_home(3, DQ_AT + 3 * DIM, DIM)
    share(2, total(1, gj, NJ), gz, z, NZ, z_peer)
    keys_home()
    for n in range(HEADS + 1):
        wait(back_out.at[:, pl.ds(n * DIM, DIM)], sem4.at[n])
    dk = turn(back_out[:, DK_AT:DV_AT].astype(F32), home_cos[...], -home_sin[...])
    back_out[:, DK_AT:DV_AT] = norm_back(dk, home_hat[...], home_inv[...], kgain)
    gain_out[...] = total(2, gz, NZ)
    wait(back_out.at[:, pl.ds(DV_AT, DIM)], sem4.at[HEADS + 1])

    wait(r1.at[pl.ds(0, ROWS - 16)], send.at[0])
    wait(s2.at[pl.ds(0, 16 - 2)], send.at[1])
    wait(s3.at[:, pl.ds(0, UNIT - 16)], send.at[2])
    wait(s4.at[pl.ds(0, ROWS - 16)], send.at[3])
    wait(kraw, send.at[4])
    wait(hr3.at[pl.ds(0, 16 - 2)], send.at[5])

    @pl.when(j == 0)
    def _():
        wait(hr3.at[pl.ds(0, 2)], send.at[6])

    wait(vraw, send.at[7])
    wait(gx.at[pl.ds(0, NX - 1)], send.at[8])
    wait(gj.at[pl.ds(0, NJ - 1)], send.at[9])
    wait(gz.at[pl.ds(0, NZ - 1)], send.at[10])


def finish(back, gains, dq, dk, dv, gain_q, gain_k, held, held_gains, sems):
    pieces = (
        (back.at[:, pl.ds(DQ_AT, HEADS * DIM)], held.at[:, pl.ds(DQ_AT, HEADS * DIM)], dq),
        (back.at[:, pl.ds(DK_AT, DIM)], held.at[:, pl.ds(DK_AT, DIM)], dk),
        (back.at[:, pl.ds(DV_AT, DIM)], held.at[:, pl.ds(DV_AT, DIM)], dv),
        (gains.at[pl.ds(0, 1)], held_gains.at[pl.ds(0, 1)], gain_q),
        (gains.at[pl.ds(1, 1)], held_gains.at[pl.ds(1, 1)], gain_k),
    )
    arriving = [
        pltpu.make_async_copy(src, mid, sems.at[0, n]) for n, (src, mid, _) in enumerate(pieces)
    ]
    leaving = [
        pltpu.make_async_copy(mid, dst, sems.at[1, n]) for n, (_, mid, dst) in enumerate(pieces)
    ]
    for copy in arriving:
        copy.start()
    for first, second in zip(arriving, leaving):
        first.wait()
        second.start()
    for copy in leaving:
        copy.wait()


def local(query_pre, key_pre, values, grad_out, query_gain, key_gain, doc_units):
    vmem = pl.BlockSpec(memory_space=pltpu.VMEM)
    dma = pltpu.SemaphoreType.DMA
    back, gains = pl.pallas_call(
        kernel,
        out_shape=[
            jax.ShapeDtypeStruct((ROWS, BACK), BF16),
            jax.ShapeDtypeStruct((2, DIM), F32),
        ],
        in_specs=[pl.BlockSpec(memory_space=pltpu.HBM)] * 7,
        out_specs=[vmem] * 2,
        scratch_shapes=[
            pltpu.VMEM((1, DIM), BF16),
            pltpu.VMEM((1, DIM), BF16),
            pltpu.VMEM((1, UNIT), jnp.int32),
            pltpu.VMEM((ROWS, FWD), BF16),
            pltpu.VMEM((16, 16, FWD), BF16),
            pltpu.VMEM((2, UNIT, FWD), BF16),
            pltpu.VMEM((2, UNIT, BACK), BF16),
            pltpu.VMEM((16, 16, BACK), BF16),
            pltpu.VMEM((ROWS, BACK), BF16),
            pltpu.VMEM((2, UNIT, DIM), BF16),
            pltpu.VMEM((2, UNIT, DIM), BF16),
            pltpu.VMEM((2, UNIT, HALO), BF16),
            pltpu.VMEM((16, 16, HALO), BF16),
            pltpu.VMEM((4 * UNIT, DIM), BF16),
            pltpu.VMEM((4 * UNIT, DIM), BF16),
            pltpu.VMEM((2, HEADS * UNIT, DIM), BF16),
            pltpu.VMEM((HEADS, 2 * UNIT, DIM), F32),
            pltpu.VMEM((HEADS, 2 * UNIT, 1), F32),
            pltpu.VMEM((4 * UNIT, DIM), F32),
            pltpu.VMEM((2, HEADS, 3 * UNIT, UNIT), F32),
            pltpu.VMEM((4 * UNIT, DIM), F32),
            pltpu.VMEM((4 * UNIT, DIM), F32),
            pltpu.VMEM((ROWS, ROWS), BF16),
            pltpu.VMEM((4 * UNIT, DIM), F32),
            pltpu.VMEM((4 * UNIT, DIM), F32),
            pltpu.VMEM((3, 2, DIM), F32),
            pltpu.VMEM((ROWS, DIM), BF16),
            pltpu.VMEM((ROWS, DIM), F32),
            pltpu.VMEM((ROWS, 1), F32),
            pltpu.VMEM((ROWS, DIM), F32),
            pltpu.VMEM((ROWS, DIM), F32),
            pltpu.VMEM((NX, 2, DIM), F32),
            pltpu.VMEM((NJ, 2, DIM), F32),
            pltpu.VMEM((NZ, 2, DIM), F32),
            dma((2 + 2 * HEADS,)),
            dma((2 + 2 * HEADS,)),
            dma((2 + HEADS,)),
            dma((2 + HEADS,)),
            dma((2,)),
            dma((3,)),
            dma((11,)),
            dma((4,)),
        ],
        compiler_params=pltpu.CompilerParams(
            collective_id=0, has_side_effects=True, vmem_limit_bytes=63 * 1024 * 1024
        ),
        cost_estimate=pl.CostEstimate(
            flops=1_300_000_000, bytes_accessed=4_000_000, transcendentals=1_000_000
        ),
    )(
        query_pre[:, 0, :],
        key_pre[:, 0, :],
        values[:, 0, :],
        grad_out[:, 0, :],
        query_gain.reshape(1, DIM),
        key_gain.reshape(1, DIM),
        doc_units.reshape(1, UNIT),
    )
    hbm = pl.BlockSpec(memory_space=pltpu.HBM)
    dq, dk, dv, gain_q, gain_k = pl.pallas_call(
        finish,
        out_shape=[
            jax.ShapeDtypeStruct((ROWS, HEADS * DIM), BF16),
            jax.ShapeDtypeStruct((ROWS, DIM), BF16),
            jax.ShapeDtypeStruct((ROWS, DIM), BF16),
            jax.ShapeDtypeStruct((1, DIM), F32),
            jax.ShapeDtypeStruct((1, DIM), F32),
        ],
        in_specs=[hbm] * 2,
        out_specs=[hbm] * 5,
        scratch_shapes=[pltpu.VMEM((ROWS, BACK), BF16), pltpu.VMEM((2, DIM), F32), dma((2, 5))],
    )(back, gains)
    return dq[:, None, :], dk[:, None, :], dv[:, None, :], gain_q[0], gain_k[0]


def solution(mesh):
    token = P(None, "dc", "tp")
    return jax.shard_map(
        local,
        mesh=mesh,
        in_specs=(token, token, token, token, P(), P(), P()),
        out_specs=(token, token, token, P(), P()),
        check_vma=False,
    )
```

```python
import math

import jax
import jax.numpy as jnp
from jax import lax
from jax.experimental import pallas as pl
from jax.experimental.pallas import tpu as pltpu
from jax.sharding import PartitionSpec as P

HEADS = 4
DIM = 128
UNIT = 128
EPS = 1e-06
THETA = 1000000.0
SCALE = 1.0 / math.sqrt(DIM)
MASKED = -1e30

NZ = 16
NJ = 8
NX = 4
AHEAD = 3
ROWS = NZ * NJ * 2

K_AT, V_AT, Q_AT, G_AT, FWD = 0, 128, 256, 768, 1280
DQ_AT, DK_AT, DV_AT, BACK = 0, 512, 640, 768
HALO = 256

MESH = pl.DeviceIdType.MESH
F32 = jnp.float32
BF16 = jnp.bfloat16


def dot(a, b, dims):
    return lax.dot_general(a, b, (dims, ((), ())), preferred_element_type=F32)


def swap_halves(x):
    return pltpu.roll(x, DIM // 2, 1)


def kernel(
    q_in, k_in, v_in, g_in, qgain_in, kgain_in, docs_in,
    back_out, gain_out,
    qgain_ref, kgain_ref, docs_ref,
    r1, s2, r2, s3, r3, s4, kraw, vraw, h3, hr3, kwin, vwin,
    qrot, qhat, qinv, khat, prob, dkacc, dvacc, perm, cosw, sinw, gpart,
    home_k, home_hat, home_inv, home_cos, home_sin,
    gx, gj, gz,
    sem1, sem2, sem3, sem4, semh, semg, send, small,
):
    me = lax.axis_index("dc")
    x = lax.axis_index("tp")
    y = me // 32
    z = lax.rem(me, 32) // 2
    c = lax.rem(me, 2)
    j = y * 2 + c
    p = z * NJ + j

    def at(yy, zz, cc):
        return (yy * 32 + zz * 2 + cc, x)

    def z_peer(i):
        i = NZ - 2 - i
        k = i // 2 + 1
        other = jnp.where((i & 1) == 0, z + k, z + NZ - k) & (NZ - 1)
        return other, at(y, other, c)

    def j_peer(i):
        k = (i + 1) // 2
        other = jnp.where((i & 1) == 0, j + NJ // 2 + k, j + NJ // 2 - k) & (NJ - 1)
        return other, at(other // 2, z, other & 1)

    def x_peer(i):
        other = (x + 1 + i) & (NX - 1)
        return other, (me, other)

    def owner(pp):
        pp = (pp + ROWS // 2) & (ROWS // 2 - 1)
        jj = pp & (NJ - 1)
        return at(jj // 2, pp // NJ, jj & 1)

    def each(count, body):
        def step(i, carry):
            body(i)
            return carry

        lax.fori_loop(0, count, step, 0, unroll=True)

    def remote(src, dst, send_sem, recv_sem, device):
        pltpu.make_async_remote_copy(
            src_ref=src, dst_ref=dst, send_sem=send_sem, recv_sem=recv_sem,
            device_id=device, device_id_type=MESH,
        ).start()

    def wait(ref, sem):
        pltpu.make_async_copy(ref, ref, sem).wait()

    for n, (src, dst) in enumerate(
        ((qgain_in, qgain_ref), (kgain_in, kgain_ref), (docs_in, docs_ref), (k_in, home_k))
    ):
        pltpu.make_async_copy(src, dst, small.at[n]).start()
    barrier = pltpu.get_barrier_semaphore()

    def greet(device):
        pl.semaphore_signal(barrier, inc=1, device_id=device, device_id_type=MESH)

    each(NZ - 1, lambda i: greet(z_peer(i)[1]))
    each(NJ - 1, lambda i: greet(j_peer(i)[1]))
    each(NX - 1, lambda i: greet(x_peer(i)[1]))
    greet(owner(p + 1))
    greet(owner(p - 1))

    @pl.when(j != 0)
    def _():
        greet(at(0, (z + 1) & (NZ - 1), 0))

    greeted = NZ - 1 + NJ - 1 + NX - 1 + 2
    pl.semaphore_wait(barrier, jnp.where(j == 0, greeted + NJ - 1, greeted))

    sources = [(k_in, 0, K_AT, DIM), (v_in, 0, V_AT, DIM)]
    sources += [(q_in, h * DIM, Q_AT + h * DIM, 2 * DIM) for h in (0, 2)]
    sources += [(g_in, h * DIM, G_AT + h * DIM, DIM) for h in range(HEADS)]

    def depart(n):
        ref, start, lane, width = sources[n]
        here = r1.at[pl.ds(pl.multiple_of(z * 16, 16), 16), pl.ds(lane, width)]

        def block(other):
            return ref.at[pl.ds(pl.multiple_of(other * 16, 16), 16), pl.ds(start, width)]

        def go(i):
            other, device = z_peer(i)
            remote(block(other), here, send.at[0], sem1.at[n], device)

        pltpu.make_async_copy(block(z), here, sem1.at[n]).start()
        each(NZ - 1, go)

    for n in range(AHEAD):
        depart(n)

    row = lax.broadcasted_iota(jnp.int32, (ROWS, ROWS), 0)
    col = lax.broadcasted_iota(jnp.int32, (ROWS, ROWS), 1)
    perm[...] = jnp.where((row % 16) * 16 + row // 16 == col, 1.0, 0.0).astype(BF16)

    wait(qgain_ref, small.at[0])
    wait(kgain_ref, small.at[1])
    wait(docs_ref, small.at[2])
    wait(home_k, small.at[3])

    lens = jnp.broadcast_to(docs_ref[...].astype(F32), (UNIT, UNIT))
    doc = lax.broadcasted_iota(jnp.int32, (UNIT, UNIT), 0)
    before = lax.broadcasted_iota(jnp.int32, (UNIT, UNIT), 1)
    starts = jnp.sum(jnp.where(before < doc, lens, 0.0), axis=1, keepdims=True)
    unit = [(2 * p + u).astype(F32) for u in range(2)]
    first = [
        jnp.max(jnp.where(starts <= unit[u], starts, 0.0), axis=0, keepdims=True)
        for u in range(2)
    ]

    def token(index):
        jj = index // 16
        return (jj // 2) * 32 + (index % 16) * 2 + jj % 2

    lane = lax.broadcasted_iota(jnp.int32, (UNIT, DIM), 1)
    place = token(lax.broadcasted_iota(jnp.int32, (UNIT, DIM), 0))
    half = DIM // 2
    freq = jnp.exp((lane % half).astype(F32) * (-2.0 * math.log(THETA) / DIM))
    sign = jnp.where(lane < half, -1.0, 1.0)
    for w in range(4):
        angle = (place.astype(F32) + (unit[0] + (w - 2.0) - first[w // 3]) * UNIT) * freq
        cosw[w * UNIT : (w + 1) * UNIT] = jnp.cos(angle)
        sinw[w * UNIT : (w + 1) * UNIT] = sign * jnp.sin(angle)

    col = lax.broadcasted_iota(jnp.int32, (UNIT, UNIT), 1)
    upper = jnp.where(doc < col, 1.0, 0.0).astype(BF16)
    starts_row = dot(lens[:8].astype(BF16), upper, ((1,), (0,)))[:1]
    for half_rows in range(2):
        here = slice(half_rows * UNIT, (half_rows + 1) * UNIT)
        units = (doc + half_rows * UNIT).astype(F32)
        begun = jnp.max(jnp.where(starts_row <= units, starts_row, 0.0), axis=1, keepdims=True)
        angle = ((units - begun) * UNIT + me.astype(F32)) * freq
        home_cos[here] = jnp.cos(angle)
        home_sin[here] = sign * jnp.sin(angle)

    causal = jnp.where(
        token(lax.broadcasted_iota(jnp.int32, (UNIT, UNIT), 0))
        <= token(lax.broadcasted_iota(jnp.int32, (UNIT, UNIT), 1)),
        0.0,
        MASKED,
    )
    seen = [
        [jnp.where(first[u] <= unit[u] - back, 0.0, MASKED) for back in (2, 1)]
        for u in range(2)
    ]
    qgain = qgain_ref[...].astype(F32)
    kgain = kgain_ref[...].astype(F32)

    def turn(a, cos, sin):
        return a * cos + swap_halves(a) * sin

    def norm(raw):
        wide = raw.astype(F32)
        inv = lax.rsqrt(jnp.mean(wide * wide, axis=1, keepdims=True) + EPS)
        return wide * inv, inv

    def norm_back(turned, hat, inv, gain):
        scaled = turned * gain
        out = inv * (scaled - hat * jnp.mean(scaled * hat, axis=1, keepdims=True))
        return out.astype(BF16)

    home_hat[...], home_inv[...] = norm(home_k[...])
    own_rows = slice(2 * UNIT, 4 * UNIT)
    own_cos, own_sin = cosw[own_rows], sinw[own_rows]

    def spread(n):
        _, _, lane, width = sources[n]
        lanes = pl.ds(lane, width)
        wait(r1.at[:, lanes], sem1.at[n])
        if n + AHEAD < len(sources):
            depart(n + AHEAD)
        moved = dot(perm[...], r1[:, lanes], ((1,), (0,))).astype(BF16)
        s2[:, :, lanes] = moved.reshape(16, 16, width)
        here = r2.at[:, pl.ds(pl.multiple_of(j * 16, 16), 16), lanes]

        def go(i):
            other, device = j_peer(i)
            remote(s2.at[pl.ds(other * 2, 2), :, lanes], here, send.at[1], sem2.at[n], device)

        pltpu.make_async_copy(s2.at[pl.ds(j * 2, 2), :, lanes], here, sem2.at[n]).start()
        each(NJ - 1, go)

    def arrived(n):
        _, _, lane, width = sources[n]
        wait(r2.at[:, :, pl.ds(lane, width)], sem2.at[n])

    def give_back(n, lane, width):
        lanes = pl.ds(lane, width)
        here = r3.at[pl.ds(j * 2, 2), :, lanes]

        def block(other):
            return s3.at[:, pl.ds(pl.multiple_of(other * 16, 16), 16), lanes]

        def go(i):
            other, device = j_peer(i)
            remote(block(other), here, send.at[2], sem3.at[n], device)

        pltpu.make_async_copy(block(j), here, sem3.at[n]).start()
        each(NJ - 1, go)

    def give_keys_back():
        lanes = pl.ds(DK_AT, HALO)
        here = r3.at[pl.ds(j * 2, 2), :, lanes]
        before = (j + NJ - 1) & (NJ - 1)
        there = hr3.at[pl.ds(before * 2, 2)]
        row = jnp.where(j == 0, z + NZ - 1, z) & (NZ - 1)

        def block(ref, other, width):
            return ref.at[:, pl.ds(pl.multiple_of(other * 16, 16), 16), width]

        def go(i):
            other, device = j_peer(i)
            remote(block(s3, other, lanes), here, send.at[2], sem3.at[HEADS], device)
            remote(block(h3, other, pl.ds(0, HALO)), there, send.at[5], sem3.at[HEADS + 1], at(other // 2, row, other & 1))

        pltpu.make_async_copy(block(s3, j, lanes), here, sem3.at[HEADS]).start()
        own = block(h3, j, pl.ds(0, HALO))

        @pl.when(j == 0)
        def _():
            remote(own, there, send.at[6], sem3.at[HEADS + 1], at(y, row, c))

        @pl.when(j != 0)
        def _():
            pltpu.make_async_copy(own, there, sem3.at[HEADS + 1]).start()

        each(NJ - 1, go)

    def keys_home():
        wait(r3.at[:, :, pl.ds(DK_AT, HALO)], sem3.at[HEADS])
        wait(hr3, sem3.at[HEADS + 1])
        total = dot(perm[...], r3[:, :, DK_AT:].reshape(ROWS, HALO), ((1,), (0,)))
        total += dot(perm[...], hr3[...].reshape(ROWS, HALO), ((1,), (0,)))
        s4[:, DK_AT:] = total.astype(BF16)
        along_z(HEADS, DK_AT, DIM)
        along_z(HEADS + 1, DV_AT, DIM)

    def send_home(n, lane, width):
        lanes = pl.ds(lane, width)
        wait(r3.at[:, :, lanes], sem3.at[n])
        moved = dot(perm[...], r3[:, :, lanes].reshape(ROWS, width), ((1,), (0,)))
        s4[:, lanes] = moved.astype(BF16)
        along_z(n, lane, width)

    def along_z(n, lane, width):
        lanes = pl.ds(lane, width)
        here = back_out.at[pl.ds(pl.multiple_of(z * 16, 16), 16), lanes]

        def block(other):
            return s4.at[pl.ds(pl.multiple_of(other * 16, 16), 16), lanes]

        def go(i):
            other, device = z_peer(i)
            remote(block(other), here, send.at[3], sem4.at[n], device)

        pltpu.make_async_copy(block(z), here, sem4.at[n]).start()
        each(NZ - 1, go)

    following = owner(p + 1)

    def window(u):
        return slice(u * UNIT, (u + 3) * UNIT)

    def head(h):
        return slice(h * DIM, (h + 1) * DIM)

    def keys():
        arrived(0)
        k_here = r2.at[:, :, pl.ds(K_AT, DIM)]
        remote(k_here, kraw, send.at[4], semh.at[0], following)
        arrived(1)
        v_here = r2.at[:, :, pl.ds(V_AT, DIM)]
        remote(v_here, vraw, send.at[7], semh.at[1], following)
        use_keys(k_here[...], own_rows)
        vwin[own_rows] = v_here[...].reshape(2 * UNIT, DIM)
        dkacc[...] = jnp.zeros_like(dkacc)
        dvacc[...] = jnp.zeros_like(dvacc)

    def use_keys(raw, rows):
        hat, _ = norm(raw.reshape(2 * UNIT, DIM))
        khat[rows] = hat
        kwin[rows] = turn(hat * kgain, cosw[rows], sinw[rows]).astype(BF16)

    def scores(h):
        if h % 2 == 0:
            arrived(2 + h // 2)
        raw = r2[:, :, Q_AT + h * DIM : Q_AT + (h + 1) * DIM].reshape(2 * UNIT, DIM)
        hat, inv = norm(raw)
        qhat[h] = hat
        qinv[h] = inv
        rot = turn(hat * qgain, own_cos, own_sin).astype(BF16)
        for u in range(2):
            qrot[u, head(h)] = rot[u * UNIT : (u + 1) * UNIT]
        if h == 0:
            wait(kraw, semh.at[0])
            use_keys(kraw[...], slice(0, 2 * UNIT))
        for u in range(2):
            s = dot(kwin[window(u)], qrot[u, head(h)], ((1,), (1,))) * SCALE
            s = jnp.concatenate(
                [
                    s[:UNIT] + seen[u][0],
                    s[UNIT : 2 * UNIT] + seen[u][1],
                    s[2 * UNIT :] + causal,
                ],
                axis=0,
            )
            e = jnp.exp(s - jnp.max(s, axis=0, keepdims=True))
            prob[u, h] = e * (1.0 / jnp.sum(e, axis=0, keepdims=True))

    def gradients(h):
        arrived(4 + h)
        if h == 0:
            wait(vraw, semh.at[1])
            vwin[: 2 * UNIT] = vraw[...].reshape(2 * UNIT, DIM)
        grads = []
        for u in range(2):
            g = r2[u, :, G_AT + h * DIM : G_AT + (h + 1) * DIM]
            att = prob[u, h]
            low = att.astype(BF16)
            datt = dot(vwin[window(u)], g, ((1,), (1,)))
            delta = jnp.sum(low.astype(F32) * datt, axis=0, keepdims=True)
            ds = (att * (datt - delta)).astype(BF16)
            dvacc[window(u)] += dot(low, g, ((1,), (0,)))
            dkacc[window(u)] += dot(ds, qrot[u, head(h)], ((1,), (0,)))
            dq = dot(ds, kwin[window(u)], ((0,), (0,))) * SCALE
            grads.append(dq.astype(BF16).astype(F32))
        turned = turn(jnp.concatenate(grads, axis=0), own_cos, -own_sin)
        out = norm_back(turned, qhat[h], qinv[h], qgain)
        s3[:, :, DQ_AT + h * DIM : DQ_AT + (h + 1) * DIM] = out.reshape(2, UNIT, DIM)
        give_back(h, DQ_AT + h * DIM, DIM)
        if h == HEADS - 1:
            dk = dkacc[...] * SCALE
            low = dk.astype(BF16).reshape(4, UNIT, DIM)
            s3[:, :, DK_AT:DV_AT] = low[2:]
            h3[:, :, :DIM] = low[:2]
            low = dvacc[...].astype(BF16).reshape(4, UNIT, DIM)
            s3[:, :, DV_AT:] = low[2:]
            h3[:, :, DIM:] = low[:2]
            give_keys_back()
            turned_k = turn(dk, cosw[...], -sinw[...])
            gpart[0, 1:2] = jnp.sum(turned_k * khat[...], axis=0, keepdims=True)
        return jnp.sum(turned * qhat[h], axis=0, keepdims=True)

    def share(stage, value, slots, mine, count, peer):
        if value is not None:
            gpart[stage] = value
        slots[mine] = gpart[stage]

        def go(i):
            remote(gpart.at[stage], slots.at[mine], send.at[8 + stage], semg.at[stage], peer(i)[1])

        each(count - 1, go)

    def total(stage, slots, count):
        wait(slots.at[pl.ds(0, count - 1)], semg.at[stage])
        return jnp.sum(slots[...], axis=0)

    q_at, g_at = 2, 4
    spread(0)
    spread(1)
    spread(q_at)
    keys()
    spread(q_at + 1)
    scores(0)
    scores(1)
    spread(g_at)
    scores(2)
    scores(3)
    spread(g_at + 1)
    qpart = gradients(0)
    spread(g_at + 2)
    qpart += gradients(1)
    spread(g_at + 3)
    send_home(0, DQ_AT, DIM)
    qpart += gradients(2)
    send_home(1, DQ_AT + DIM, DIM)
    qpart += gradients(3)
    gpart[0, 0:1] = qpart
    share(0, None, gx, x, NX, x_peer)
    send_home(2, DQ_AT + 2 * DIM, DIM)
    share(1, total(0, gx, NX), gj, j, NJ, j_peer)
    send_home(3, DQ_AT + 3 * DIM, DIM)
    share(2, total(1, gj, NJ), gz, z, NZ, z_peer)
    keys_home()
    for n in range(HEADS + 1):
        wait(back_out.at[:, pl.ds(n * DIM, DIM)], sem4.at[n])
    dk = turn(back_out[:, DK_AT:DV_AT].astype(F32), home_cos[...], -home_sin[...])
    back_out[:, DK_AT:DV_AT] = norm_back(dk, home_hat[...], home_inv[...], kgain)
    gain_out[...] = total(2, gz, NZ)
    wait(back_out.at[:, pl.ds(DV_AT, DIM)], sem4.at[HEADS + 1])

    wait(r1.at[pl.ds(0, ROWS - 16)], send.at[0])
    wait(s2.at[pl.ds(0, 16 - 2)], send.at[1])
    wait(s3.at[:, pl.ds(0, UNIT - 16)], send.at[2])
    wait(s4.at[pl.ds(0, ROWS - 16)], send.at[3])
    wait(kraw, send.at[4])
    wait(hr3.at[pl.ds(0, 16 - 2)], send.at[5])

    @pl.when(j == 0)
    def _():
        wait(hr3.at[pl.ds(0, 2)], send.at[6])

    wait(vraw, send.at[7])
    wait(gx.at[pl.ds(0, NX - 1)], send.at[8])
    wait(gj.at[pl.ds(0, NJ - 1)], send.at[9])
    wait(gz.at[pl.ds(0, NZ - 1)], send.at[10])


def finish(back, gains, dq, dk, dv, gain_q, gain_k, held, held_gains, sems):
    pieces = (
        (back.at[:, pl.ds(DQ_AT, HEADS * DIM)], held.at[:, pl.ds(DQ_AT, HEADS * DIM)], dq),
        (back.at[:, pl.ds(DK_AT, DIM)], held.at[:, pl.ds(DK_AT, DIM)], dk),
        (back.at[:, pl.ds(DV_AT, DIM)], held.at[:, pl.ds(DV_AT, DIM)], dv),
        (gains.at[pl.ds(0, 1)], held_gains.at[pl.ds(0, 1)], gain_q),
        (gains.at[pl.ds(1, 1)], held_gains.at[pl.ds(1, 1)], gain_k),
    )
    arriving = [
        pltpu.make_async_copy(src, mid, sems.at[0, n]) for n, (src, mid, _) in enumerate(pieces)
    ]
    leaving = [
        pltpu.make_async_copy(mid, dst, sems.at[1, n]) for n, (_, mid, dst) in enumerate(pieces)
    ]
    for copy in arriving:
        copy.start()
    for first, second in zip(arriving, leaving):
        first.wait()
        second.start()
    for copy in leaving:
        copy.wait()


def local(query_pre, key_pre, values, grad_out, query_gain, key_gain, doc_units):
    vmem = pl.BlockSpec(memory_space=pltpu.VMEM)
    dma = pltpu.SemaphoreType.DMA
    back, gains = pl.pallas_call(
        kernel,
        out_shape=[
            jax.ShapeDtypeStruct((ROWS, BACK), BF16),
            jax.ShapeDtypeStruct((2, DIM), F32),
        ],
        in_specs=[pl.BlockSpec(memory_space=pltpu.HBM)] * 7,
        out_specs=[vmem] * 2,
        scratch_shapes=[
            pltpu.VMEM((1, DIM), BF16),
            pltpu.VMEM((1, DIM), BF16),
            pltpu.VMEM((1, UNIT), jnp.int32),
            pltpu.VMEM((ROWS, FWD), BF16),
            pltpu.VMEM((16, 16, FWD), BF16),
            pltpu.VMEM((2, UNIT, FWD), BF16),
            pltpu.VMEM((2, UNIT, BACK), BF16),
            pltpu.VMEM((16, 16, BACK), BF16),
            pltpu.VMEM((ROWS, BACK), BF16),
            pltpu.VMEM((2, UNIT, DIM), BF16),
            pltpu.VMEM((2, UNIT, DIM), BF16),
            pltpu.VMEM((2, UNIT, HALO), BF16),
            pltpu.VMEM((16, 16, HALO), BF16),
            pltpu.VMEM((4 * UNIT, DIM), BF16),
            pltpu.VMEM((4 * UNIT, DIM), BF16),
            pltpu.VMEM((2, HEADS * UNIT, DIM), BF16),
            pltpu.VMEM((HEADS, 2 * UNIT, DIM), F32),
            pltpu.VMEM((HEADS, 2 * UNIT, 1), F32),
            pltpu.VMEM((4 * UNIT, DIM), F32),
            pltpu.VMEM((2, HEADS, 3 * UNIT, UNIT), F32),
            pltpu.VMEM((4 * UNIT, DIM), F32),
            pltpu.VMEM((4 * UNIT, DIM), F32),
            pltpu.VMEM((ROWS, ROWS), BF16),
            pltpu.VMEM((4 * UNIT, DIM), F32),
            pltpu.VMEM((4 * UNIT, DIM), F32),
            pltpu.VMEM((3, 2, DIM), F32),
            pltpu.VMEM((ROWS, DIM), BF16),
            pltpu.VMEM((ROWS, DIM), F32),
            pltpu.VMEM((ROWS, 1), F32),
            pltpu.VMEM((ROWS, DIM), F32),
            pltpu.VMEM((ROWS, DIM), F32),
            pltpu.VMEM((NX, 2, DIM), F32),
            pltpu.VMEM((NJ, 2, DIM), F32),
            pltpu.VMEM((NZ, 2, DIM), F32),
            dma((2 + 2 * HEADS,)),
            dma((2 + 2 * HEADS,)),
            dma((2 + HEADS,)),
            dma((2 + HEADS,)),
            dma((2,)),
            dma((3,)),
            dma((11,)),
            dma((4,)),
        ],
        compiler_params=pltpu.CompilerParams(
            collective_id=0, has_side_effects=True, vmem_limit_bytes=63 * 1024 * 1024
        ),
        cost_estimate=pl.CostEstimate(
            flops=1_300_000_000, bytes_accessed=4_000_000, transcendentals=1_000_000
        ),
    )(
        query_pre[:, 0, :],
        key_pre[:, 0, :],
        values[:, 0, :],
        grad_out[:, 0, :],
        query_gain.reshape(1, DIM),
        key_gain.reshape(1, DIM),
        doc_units.reshape(1, UNIT),
    )
    hbm = pl.BlockSpec(memory_space=pltpu.HBM)
    dq, dk, dv, gain_q, gain_k = pl.pallas_call(
        finish,
        out_shape=[
            jax.ShapeDtypeStruct((ROWS, HEADS * DIM), BF16),
            jax.ShapeDtypeStruct((ROWS, DIM), BF16),
            jax.ShapeDtypeStruct((ROWS, DIM), BF16),
            jax.ShapeDtypeStruct((1, DIM), F32),
            jax.ShapeDtypeStruct((1, DIM), F32),
        ],
        in_specs=[hbm] * 2,
        out_specs=[hbm] * 5,
        scratch_shapes=[pltpu.VMEM((ROWS, BACK), BF16), pltpu.VMEM((2, DIM), F32), dma((2, 5))],
    )(back, gains)
    return dq[:, None, :], dk[:, None, :], dv[:, None, :], gain_q[0], gain_k[0]


def solution(mesh):
    token = P(None, "dc", "tp")
    return jax.shard_map(
        local,
        mesh=mesh,
        in_specs=(token, token, token, token, P(), P(), P()),
        out_specs=(token, token, token, P(), P()),
        check_vma=False,
    )
```
